128 devices in a mesh: dp: 32 (over z, y, core), mp: 4 (over x).
Axes of the slice: x: 4, y: 4, z: 4, core: 2. Of those that a mesh axis runs over, the one named last changes fastest.
Arguments:
- features: bfloat16 [262144, 512], P('dp', 'mp'), may hold values from -6 to 6
- conv6_weight: bfloat16 [1024, 512], P('dp', 'mp'), may hold values from -0.1875 to 0.1875
- conv7_weight: bfloat16 [1024, 512], P('dp', 'mp'), may hold values from -0.1875 to 0.1875
- frame_grads: bfloat16 [65536, 512], P('dp', 'mp'), may hold values from -0.29882812 to 0.29882812
- frame_dest: int32 [65536], replicated, may hold values from 0 to 65535, as said below
- lengths: int32 [128], P('dp'), may hold values from 41360 to 163920
Outputs:
- grad_features: bfloat16 [262144, 512], P('dp', 'mp')
- grad_conv6: float32 [1024, 512], P('dp', 'mp')
- grad_conv7: float32 [1024, 512], P('dp', 'mp')
The draws below stay inside these ranges and needn't reach their ends.
Inputs may be any that keep to these rules, and one draw needn't show every extreme that they name: frame_dest maps the packed slots one to one onto all waveform frames; frame f belongs to the waveform owner f // 2048, slot j lies on transformer owner j // 2048. Every transformer owner sends at most 192 frames to one waveform owner and exactly 192 to one of them; every waveform owner receives exactly 192 frames from one transformer owner. `lengths`: entry d * 4 + u belongs to the utterance in output frames (d * 4 + u) * 512 onward.
All inputs are finite; a program needn't handle non-finite values.
Results may differ from the reference program's by a relative error of at most 0.006.
Values may be sent and summed in bfloat16 or wider, within the bound.
A program may use at most 128 MiB of HBM per device.

```python
import jax
import jax.numpy as jnp
from jax import lax

C = 512
FRM_DEV = 2048
UTT_DEV = 4
MAXF = 512
FRAMES = 65536
CAP = 192
N_DP = 32


def draw_frame_dest(key, part):
    keys = jax.random.split(jax.random.fold_in(key, 17), 5)
    dp_count = N_DP
    frames = FRM_DEV
    base = jnp.concatenate([jnp.zeros((CAP,), jnp.int32), 1 + jnp.arange(frames - CAP, dtype=jnp.int32) % (dp_count - 1)])
    offsets = jax.random.permutation(keys[0], base)
    owner_perm = jax.random.permutation(keys[1], dp_count)
    source_perm = jax.random.permutation(keys[2], dp_count)
    row_perm = jax.random.permutation(keys[3], frames)
    row_shift = jax.random.randint(keys[4], (dp_count,), 0, frames)
    sources = jnp.arange(dp_count, dtype=jnp.int32)[:, None]
    owners = owner_perm[(source_perm[sources] + offsets[None, :]) % dp_count]
    rows = (row_perm[None, :] + row_shift[owners]) % frames
    return (owners * frames + rows).reshape(-1).astype(jnp.int32)


def plant(result, own_key, smallest, top_value):
    dims = result.shape
    place = [jax.random.randint(jax.random.fold_in(own_key, axis), (), 0, dims[axis]) for axis in range(len(dims))]
    result = result.at[tuple(place)].set(smallest)
    longest = dims.index(max(dims))
    place[longest] = (place[longest] + 1) % dims[longest]
    return result.at[tuple(place)].set(top_value)


def shard_levels(rng, extent, cuts, least, top_value):
    level, own = 1.0, jax.random.fold_in(rng, 6)
    for axis_at, blocks in cuts:
        steps = jnp.exp(jax.random.uniform(jax.random.fold_in(own, axis_at), (blocks,), jnp.float32, least / len(cuts), top_value / len(cuts)))
        level = level * jnp.repeat(steps, extent[axis_at] // blocks).reshape([-1 if axis == axis_at else 1 for axis in range(len(extent))])
    return level


def centred(rng, dims, deviation, reach, cuts=(), kind=jnp.bfloat16):
    drawn = jax.random.normal(rng, dims, jnp.float32) * deviation
    if len(cuts) > 0:
        drawn = shard_levels(rng, dims, cuts, -0.22, 0.18) * drawn
    return jnp.clip(drawn, min=-reach, max=reach).astype(kind)


def setup_inputs(seed: int = 0) -> dict:
    key_of = jax.random.split(jax.random.key(seed), 7)
    features = centred(key_of[0], (4 * FRAMES, C), 1.0, 6.0, ((0, 32), (1, 4)))
    conv6_weight = centred(key_of[1], (2 * C, C), (2 * C) ** -0.5, 0.1875, ((0, 32), (1, 4)))
    conv7_weight = centred(key_of[2], (2 * C, C), (2 * C) ** -0.5, 0.1875, ((0, 32), (1, 4)))
    frame_grads = centred(key_of[3], (FRAMES, C), 0.05, 0.29882812, ((0, 32), (1, 4)))
    frame_dest = draw_frame_dest(jax.random.fold_in(key_of[6], 71), 0)
    lengths = plant(jax.random.randint(key_of[5], (N_DP * UTT_DEV,), 400 + 320 * (MAXF // 4), 401 + 320 * (MAXF - 1)), jax.random.fold_in(key_of[5], 1), 400 + 320 * (MAXF // 4), (401 + 320 * (MAXF - 1)) - 1).astype(jnp.int32)
    return dict(features=features, conv6_weight=conv6_weight, conv7_weight=conv7_weight, frame_grads=frame_grads, frame_dest=frame_dest, lengths=lengths)


inv_root_two = 0.7071067811865476
inv_root_tau = 0.3989422804014327


def gelu_exact(values):
    return 0.5 * values * (1.0 + jax.scipy.special.erf(values * inv_root_two))


def gelu_slope(values):
    return 0.5 * (1.0 + jax.scipy.special.erf(values * inv_root_two)) + values * jnp.exp(-0.5 * values * values) * inv_root_tau


def transposed(left, right):
    return lax.dot_general(left, right, (((0,), (0,)), ((), ())), preferred_element_type=jnp.float32)


def reference(features, conv6_weight, conv7_weight, frame_grads, frame_dest, lengths):
    total = frame_grads.shape[0]
    routed = jnp.zeros(frame_grads.shape, jnp.bfloat16).at[frame_dest].set(frame_grads)
    valid_frames = (lengths - 400) // 320 + 1
    positions = jnp.arange(total, dtype=jnp.int32)
    limits = jnp.repeat(valid_frames, MAXF, total_repeat_length=total)
    masked = jnp.where((positions % MAXF < limits)[:, None], routed, jnp.zeros_like(routed))
    in_pairs = features.reshape(2 * total, 2 * C)
    pre_six = jnp.dot(in_pairs, conv6_weight, preferred_element_type=jnp.float32)
    act_six = gelu_exact(pre_six).astype(jnp.bfloat16)
    six_pairs = act_six.reshape(total, 2 * C)
    pre_seven = jnp.dot(six_pairs, conv7_weight, preferred_element_type=jnp.float32)
    delta_seven = (masked.astype(jnp.float32) * gelu_slope(pre_seven)).astype(jnp.bfloat16)
    grad_conv7 = transposed(six_pairs, delta_seven)
    back_six = lax.dot_general(delta_seven, conv7_weight, (((1,), (1,)), ((), ())), preferred_element_type=jnp.float32).reshape(2 * total, C)
    delta_six = (back_six * gelu_slope(pre_six)).astype(jnp.bfloat16)
    grad_conv6 = transposed(in_pairs, delta_six)
    back_in = lax.dot_general(delta_six, conv6_weight, (((1,), (1,)), ((), ())), preferred_element_type=jnp.float32)
    grad_features = back_in.reshape(4 * total, C).astype(jnp.bfloat16)
    return grad_features, grad_conv6, grad_conv7
```

```python
import jax
import jax.numpy as jnp
from jax import lax
from jax.experimental import pallas as pl
from jax.experimental.pallas import tpu as pltpu
from jax.sharding import PartitionSpec as P

C = 512
FRM = 2048
CAP = 192
N_DP = 32
N_MP = 4
CH = C // N_MP
UTT = FRM // N_MP
FC = 128
NCH = UTT // FC
RC = 4 * FC
META = 16
BLK = CAP + META
SLOT = 256
GRP = 4
KR = 32
NQ = N_DP // 2

inv_root_two = 0.7071067811865476
inv_root_tau = 0.3989422804014327
F32 = jnp.float32
BF16 = jnp.bfloat16


def dot(left, right, contract=((1,), (0,))):
    return lax.dot_general(left, right, (contract, ((), ())), preferred_element_type=F32)


def iota(shape, axis):
    return lax.broadcasted_iota(jnp.int32, shape, axis)


def kernel(
    feat, w6, w7, grads, dest, lens,
    gf, g6, g7,
    xin, wts, rank, rhs, obox, arrived, placed, exb, mg,
    s32, pairs6, pairs7, slope6, slope7, delta7, delta6, gout,
    gsum, core_out, core_in, chip_in, chip_out, share, x_out, x_in,
    wx_s, wx_r, wy_s, wy_r, wc_s, wc_r, own_sem, f_s, f_r, rt_s, rt_r, ex_s, ex_r,
    go_s, go_r, rc_s, rc_r, ry_s, ry_r, rx_s, rx_r,
):
    d, m = lax.axis_index("dp"), lax.axis_index("mp")
    core, q = lax.rem(d, 2), lax.div(d, 2)
    mate = d + 1 - 2 * core

    def remote(src, dst, send, recv, dp, mp):
        return pltpu.make_async_remote_copy(
            src_ref=src, dst_ref=dst, send_sem=send, recv_sem=recv,
            device_id=(dp, mp), device_id_type=pl.DeviceIdType.MESH,
        )

    barrier = pltpu.get_barrier_semaphore()

    @pl.loop(1, N_DP)
    def _(k):
        pl.semaphore_signal(barrier, inc=1, device_id=(lax.rem(d + k, N_DP), m), device_id_type=pl.DeviceIdType.MESH)

    for i in range(1, N_MP):
        pl.semaphore_signal(barrier, inc=1, device_id=(d, lax.rem(m + i, N_MP)), device_id_type=pl.DeviceIdType.MESH)
    pl.semaphore_wait(barrier, N_DP - 1 + N_MP - 1)

    cols = pl.ds(pl.multiple_of(m * CH, CH), CH)
    wts[0, q, core, :, cols] = w6[...]
    wts[1, q, core, :, cols] = w7[...]

    def wx(i, w):
        block = wts.at[w, q, core, :, cols]
        return remote(block, block, wx_s.at[i, w], wx_r.at[i, w], d, lax.rem(m + i, N_MP))

    for i in range(1, N_MP):
        for w in range(2):
            wx(i, w).start()

    def feature(c, i):
        p = lax.rem(m + i, N_MP)
        return remote(
            feat.at[pl.ds(pl.multiple_of(p * 4 * UTT + c * RC, RC), RC), :],
            xin.at[m, pl.ds(pl.multiple_of(c * RC, RC), RC), :],
            f_s.at[c, i], f_r.at[c, i], d, p,
        )

    own_rows = pltpu.make_async_copy(
        feat.at[pl.ds(pl.multiple_of(m * 4 * UTT, 4 * UTT), 4 * UTT), :], xin.at[m], own_sem.at[0]
    )
    own_rows.start()

    for c in range(NCH):
        for i in range(1, N_MP):
            feature(c, i).start()

    target = dest[...]
    owner, row = lax.shift_right_logical(target, 11), lax.bitwise_and(target, FRM - 1)
    before = jnp.where(iota((256, 256), 0) < iota((256, 256), 1), 1.0, 0.0).astype(BF16)
    carry = jnp.zeros((N_DP, 1), F32)
    for b in range(FRM // 256):
        mine = owner[:, b * 256 : (b + 1) * 256] == iota((N_DP, 256), 0)
        ones = jnp.where(mine, 1.0, 0.0)
        earlier = dot(ones.astype(BF16), before) + carry
        rank[:, b * 256 : (b + 1) * 256] = jnp.where(mine, earlier.astype(jnp.int32), 4096)
        carry = carry + jnp.sum(ones, axis=1, keepdims=True)
    high, low = lax.shift_right_logical(row, 8), lax.bitwise_and(row, 255)
    rhs[:, 0:CH] = grads[...]
    for b in range(FRM // 128):
        part = slice(b * 128, (b + 1) * 128)
        line = iota((128, 128), 0)
        digits = jnp.where(line == 0, high[:, part], jnp.where(line == 1, low[:, part], 0))
        rhs[part, CH : 2 * CH] = digits.astype(F32).T.astype(BF16)

    for i in range(1, N_MP):
        for w in range(2):
            wx(i, w).wait()

    def wy(k):
        block = wts.at[:, q, core]
        return remote(block, block, wy_s.at[k], wy_r.at[k], 2 * lax.rem(q + k, NQ) + core, m)

    @pl.loop(1, NQ)
    def _(k):
        wy(k).start()

    def routed(k):
        return remote(
            obox.at[k], arrived.at[k, pl.ds(0, BLK), :], rt_s.at[k], rt_r.at[k], lax.rem(d + k, N_DP), m
        )

    arrived[:, BLK:SLOT, :] = jnp.zeros((N_DP, SLOT - BLK, CH), BF16)

    def pack(k):
        o = lax.rem(d + k, N_DP)
        pick = jnp.where(iota((CAP, FRM), 0) == rank[pl.ds(o, 1), :], 1.0, 0.0).astype(BF16)
        both = dot(pick, rhs[...])
        obox[k, 0:CAP, :] = both[:, :CH].astype(BF16)
        digits = jnp.concatenate([both[:, CH:], jnp.zeros((SLOT - CAP, CH), F32)], axis=0).T
        obox[k, CAP:BLK, :] = jnp.concatenate([digits[0:8, 0:128], digits[0:8, 128:256]], axis=0).astype(BF16)

    @pl.loop(1, N_DP)
    def _(k):
        pack(k)
        routed(k).start()

    pack(0)
    arrived[0, 0:BLK, :] = obox[0]

    @pl.loop(1, NQ)
    def _(k):
        wy(k).wait()

    def wc(w):
        block = wts.at[w, :, core]
        return remote(block, block, wc_s.at[w], wc_r.at[w], mate, m)

    for w in range(2):
        wc(w).start()

    def place(g):
        targets = []
        for i in range(GRP):
            digits = arrived[g * GRP + i, CAP:BLK, :].astype(F32)
            targets += [
                digits[0:1] * 256.0 + digits[1:2],
                jnp.where(iota((1, 128), 1) < CAP - 128, digits[8:9] * 256.0 + digits[9:10], -1.0),
            ]
        at = jnp.concatenate(targets, axis=1).astype(jnp.int32)
        block = arrived[pl.ds(g * GRP, GRP)].reshape(GRP * SLOT, CH)

        @pl.loop(0, N_MP)
        def _(p):
            pick = jnp.where(iota((UTT, GRP * SLOT), 0) == at - p * UTT, 1.0, 0.0).astype(BF16)
            placed[p] += dot(pick, block)

    placed[...] = jnp.zeros((N_MP, UTT, CH), F32)
    for w in range(2):
        wc(w).wait()
    own_rows.wait()

    def forward(c):
        rows = pl.ds(pl.multiple_of(c * RC, RC), RC)
        for g in range(N_MP):
            s32[g] = xin[g, rows, :].astype(F32)
        for j in range(4):
            for g in range(N_MP):
                lanes = slice((j % 2) * C + g * CH, (j % 2) * C + (g + 1) * CH)
                pairs6[c, (j // 2) * FC : (j // 2 + 1) * FC, lanes] = s32[g, pl.ds(j, FC, stride=4), :].astype(BF16)
        pre = dot(pairs6[c], wts[0].reshape(2 * C, C))
        half = 0.5 * (1.0 + lax.erf(pre * inv_root_two))
        act = (pre * half).astype(BF16)
        slope6[c] = half + pre * jnp.exp(-0.5 * pre * pre) * inv_root_tau
        pairs7[c, :, 0:C] = act[:FC]
        pairs7[c, :, C : 2 * C] = act[FC:]
        pre = dot(pairs7[c], wts[1].reshape(2 * C, C))
        half = 0.5 * (1.0 + lax.erf(pre * inv_root_two))
        slope7[c] = half + pre * jnp.exp(-0.5 * pre * pre) * inv_root_tau

    @pl.loop(0, NCH)
    def _(c):
        for i in range(1, N_MP):
            feature(c, i).wait()
        forward(c)

    for i in range(1, GRP):
        routed(i).wait()
    place(0)

    @pl.loop(1, N_DP // GRP)
    def _(g):
        for i in range(GRP):
            routed(g * GRP + i).wait()
        place(g)

    def exchange(i):
        p = lax.rem(m + i, N_MP)
        return remote(exb.at[p], mg.at[m], ex_s.at[i], ex_r.at[i], d, p)

    exb[...] = placed[...].astype(BF16)
    for i in range(1, N_MP):
        exchange(i).start()
    mg[m] = exb[m]
    for i in range(1, N_MP):
        exchange(i).wait()

    valid = lax.div(lens[m] - 400, 320) + 1

    def given(c, i):
        p = lax.rem(m + i, N_MP)
        return remote(
            gout.at[p, pl.ds(pl.multiple_of(c * RC, RC), RC), :],
            gf.at[pl.ds(pl.multiple_of(m * 4 * UTT + c * RC, RC), RC), :],
            go_s.at[c, i], go_r.at[c, i], d, p,
        )

    def own_given(c):
        return pltpu.make_async_copy(
            gout.at[m, pl.ds(pl.multiple_of(c * RC, RC), RC), :],
            gf.at[pl.ds(pl.multiple_of(m * 4 * UTT + c * RC, RC), RC), :],
            go_s.at[c, 0],
        )

    @pl.loop(0, NCH)
    def _(c):
        frames = pl.ds(pl.multiple_of(c * FC, FC), FC)
        live = iota((FC, CH), 0) + c * FC < valid
        for g in range(N_MP):
            lanes = slice(g * CH, (g + 1) * CH)
            coming = jnp.where(live, mg[g, frames, :].astype(F32), 0.0)
            delta7[c, :, lanes] = (coming * slope7[c, :, lanes]).astype(BF16)
        back = dot(delta7[c], wts[1].reshape(2 * C, C), ((1,), (1,)))
        delta6[c, 0:FC, :] = (back[:, :C] * slope6[c, 0:FC, :]).astype(BF16)
        delta6[c, FC : 2 * FC, :] = (back[:, C:] * slope6[c, FC : 2 * FC, :]).astype(BF16)
        back = dot(delta6[c], wts[0].reshape(2 * C, C), ((1,), (1,)))
        for j in range(4):
            for g in range(N_MP):
                s32[g, pl.ds(j, FC, stride=4), :] = back[
                    (j // 2) * FC : (j // 2 + 1) * FC, (j % 2) * C + g * CH : (j % 2) * C + (g + 1) * CH
                ]
        for g in range(N_MP):
            gout[g, pl.ds(pl.multiple_of(c * RC, RC), RC), :] = s32[g].astype(BF16)
        for i in range(1, N_MP):
            given(c, i).start()
        own_given(c).start()

    @pl.loop(0, 2 * C // 256)
    def _(b):
        lanes = pl.ds(pl.multiple_of(b * 256, 256), 256)
        blocks = pl.ds(b * 4, 4)
        left = pairs7[:, :, lanes].reshape(UTT, 256)
        right = delta7[...].reshape(UTT, C)
        gsum[1, blocks] = dot(left, right, ((0,), (0,))).reshape(4, 2, KR, C)
        left = pairs6[:, :, lanes].reshape(2 * UTT, 256)
        right = delta6[...].reshape(2 * UTT, C)
        gsum[0, blocks] = dot(left, right, ((0,), (0,))).reshape(4, 2, KR, C)

    core_out[...] = gsum[:, :, 1 - core].astype(BF16)
    to_mate = remote(core_out, core_in, rc_s.at[0], rc_r.at[0], mate, m)
    to_mate.start()
    to_mate.wait()

    def chips(k):
        o = lax.rem(q + k, NQ)
        return remote(chip_out.at[o], chip_in.at[k], ry_s.at[k], ry_r.at[k], 2 * o + core, m)

    @pl.loop(0, NQ)
    def _(o):
        for w in range(2):
            chip_out[o, w] = (gsum[w, o, core] + core_in[w, o].astype(F32)).astype(BF16)

    @pl.loop(1, NQ)
    def _(k):
        chips(k).start()

    for w in range(2):
        share[w] = gsum[w, q, core] + core_in[w, q].astype(F32)

    @pl.loop(1, NQ)
    def _(k):
        chips(k).wait()
        share[...] += chip_in[k].astype(F32)

    for g in range(N_MP):
        x_out[g] = share[:, :, g * CH : (g + 1) * CH].astype(BF16)

    def along(i):
        p = lax.rem(m + i, N_MP)
        return remote(x_out.at[p], x_in.at[i], rx_s.at[i], rx_r.at[i], d, p)

    for i in range(1, N_MP):
        along(i).start()
    total = jnp.zeros((2, KR, CH), F32)
    for g in range(N_MP):
        total = jnp.where(m == g, share[:, :, g * CH : (g + 1) * CH], total)
    for i in range(1, N_MP):
        along(i).wait()
        total = total + x_in[i].astype(F32)
    g6[...] = total[0]
    g7[...] = total[1]

    @pl.loop(0, NCH)
    def _(c):
        for i in range(1, N_MP):
            given(c, i).wait()
        own_given(c).wait()


def body(features, conv6_weight, conv7_weight, frame_grads, frame_dest, lengths):
    d = lax.axis_index("dp")
    own = lax.dynamic_slice_in_dim(frame_dest, d * FRM, FRM, 0).reshape(1, FRM)
    vmem, hbm = pl.BlockSpec(memory_space=pltpu.VMEM), pl.BlockSpec(memory_space=pl.ANY)
    dma = pltpu.SemaphoreType.DMA
    return pl.pallas_call(
        kernel,
        out_shape=(
            jax.ShapeDtypeStruct(features.shape, BF16),
            jax.ShapeDtypeStruct(conv6_weight.shape, F32),
            jax.ShapeDtypeStruct(conv7_weight.shape, F32),
        ),
        in_specs=[hbm, vmem, vmem, vmem, vmem, pl.BlockSpec(memory_space=pltpu.SMEM)],
        out_specs=(hbm, vmem, vmem),
        scratch_shapes=[
            pltpu.VMEM((N_MP, 4 * UTT, CH), BF16),
            pltpu.VMEM((2, NQ, 2, KR, C), BF16),
            pltpu.VMEM((N_DP, FRM), jnp.int32),
            pltpu.VMEM((FRM, 2 * CH), BF16),
            pltpu.VMEM((N_DP, BLK, CH), BF16),
            pltpu.VMEM((N_DP, SLOT, CH), BF16),
            pltpu.VMEM((N_MP, UTT, CH), F32),
            pltpu.VMEM((N_MP, UTT, CH), BF16),
            pltpu.VMEM((N_MP, UTT, CH), BF16),
            pltpu.VMEM((N_MP, RC, CH), F32),
            pltpu.VMEM((NCH, 2 * FC, 2 * C), BF16),
            pltpu.VMEM((NCH, FC, 2 * C), BF16),
            pltpu.VMEM((NCH, 2 * FC, C), F32),
            pltpu.VMEM((NCH, FC, C), F32),
            pltpu.VMEM((NCH, FC, C), BF16),
            pltpu.VMEM((NCH, 2 * FC, C), BF16),
            pltpu.VMEM((N_MP, 4 * UTT, CH), BF16),
            pltpu.VMEM((2, NQ, 2, KR, C), F32),
            pltpu.VMEM((2, NQ, KR, C), BF16),
            pltpu.VMEM((2, NQ, KR, C), BF16),
            pltpu.VMEM((NQ, 2, KR, C), BF16),
            pltpu.VMEM((NQ, 2, KR, C), BF16),
            pltpu.VMEM((2, KR, C), F32),
            pltpu.VMEM((N_MP, 2, KR, CH), BF16),
            pltpu.VMEM((N_MP, 2, KR, CH), BF16),
            dma((N_MP, 2)), dma((N_MP, 2)), dma((NQ,)), dma((NQ,)), dma((2,)), dma((2,)), dma((1,)),
            dma((NCH, N_MP)), dma((NCH, N_MP)), dma((N_DP,)), dma((N_DP,)), dma((N_MP,)), dma((N_MP,)),
            dma((NCH, N_MP)), dma((NCH, N_MP)), dma((1,)), dma((1,)), dma((NQ,)), dma((NQ,)),
            dma((N_MP,)), dma((N_MP,)),
        ],
        compiler_params=pltpu.CompilerParams(
            collective_id=0, has_side_effects=True, vmem_limit_bytes=56 * 2**20,
            fuse_transposed_lhs_in_matmul=True,
        ),
        name="encoder_backward",
    )(features, conv6_weight, conv7_weight, frame_grads, own, lengths)


def solution(mesh):
    placed = (P("dp", "mp"), P("dp", "mp"), P("dp", "mp"), P("dp", "mp"), P(), P("dp"))
    return jax.shard_map(
        body,
        mesh=mesh,
        in_specs=placed,
        out_specs=(P("dp", "mp"), P("dp", "mp"), P("dp", "mp")),
        check_vma=False,
    )
```

```python
import jax
import jax.numpy as jnp
from jax import lax
from jax.experimental import pallas as pl
from jax.experimental.pallas import tpu as pltpu
from jax.sharding import PartitionSpec as P

C = 512
FRM = 2048
CAP = 192
N_DP = 32
N_MP = 4
CH = C // N_MP
UTT = FRM // N_MP
FC = 128
NCH = UTT // FC
RC = 4 * FC
META = 16
BLK = CAP + META
KR = 32

inv_root_two = 0.7071067811865476
inv_root_tau = 0.3989422804014327
F32 = jnp.float32
BF16 = jnp.bfloat16


def dot(left, right, contract=((1,), (0,))):
    return lax.dot_general(left, right, (contract, ((), ())), preferred_element_type=F32)


def iota(shape, axis):
    return lax.broadcasted_iota(jnp.int32, shape, axis)


def kernel(
    feat, w6, w7, grads, dest, lens,
    gf, g6, g7,
    xin, wts, quad, meta, rhs, obox, arrived, placed, exb, mg,
    s32, pairs6, pairs7, slope6, slope7, delta7, delta6, gout,
    gsum, core_out, core_in, part_out, part_in, part, chip_out, chip_in, share, x_out, x_in,
    wx_s, wx_r, wa_s, wa_r, wb_s, wb_r, wc_s, wc_r, own_sem, f_s, f_r, rt_s, rt_r, ex_s, ex_r,
    go_s, go_r, rc_s, rc_r, ra_s, ra_r, rb_s, rb_r, rx_s, rx_r,
):
    d, m = lax.axis_index("dp"), lax.axis_index("mp")
    z, y, core = lax.div(d, 8), lax.rem(lax.div(d, 2), 4), lax.rem(d, 2)

    def dp_of(dz, dy, dc):
        return lax.rem(z + dz, 4) * 8 + lax.rem(y + dy, 4) * 2 + lax.rem(core + dc, 2)

    def remote(src, dst, send, recv, dp, mp):
        return pltpu.make_async_remote_copy(
            src_ref=src, dst_ref=dst, send_sem=send, recv_sem=recv,
            device_id=(dp, mp), device_id_type=pl.DeviceIdType.MESH,
        )

    barrier = pltpu.get_barrier_semaphore()
    for i in range(1, N_MP):
        pl.semaphore_signal(barrier, inc=1, device_id=(d, lax.rem(m + i, N_MP)), device_id_type=pl.DeviceIdType.MESH)

    @pl.loop(1, N_DP)
    def _(k):
        pl.semaphore_signal(barrier, inc=1, device_id=(lax.rem(d + k, N_DP), m), device_id_type=pl.DeviceIdType.MESH)

    own_rows = pltpu.make_async_copy(
        feat.at[pl.ds(pl.multiple_of(m * 4 * UTT, 4 * UTT), 4 * UTT), :], xin.at[m], own_sem.at[0]
    )
    own_rows.start()
    cols = pl.ds(pl.multiple_of(m * CH, CH), CH)
    wts[0, z, y, core, :, cols] = w6[...]
    wts[1, z, y, core, :, cols] = w7[...]
    pl.semaphore_wait(barrier, N_DP - 1 + N_MP - 1)

    def wx(i, w):
        block = wts.at[w, z, y, core, :, cols]
        return remote(block, block, wx_s.at[i, w], wx_r.at[i, w], d, lax.rem(m + i, N_MP))

    for i in range(1, N_MP):
        for w in range(2):
            wx(i, w).start()

    def feature(c, i):
        p = lax.rem(m + i, N_MP)
        return remote(
            feat.at[pl.ds(pl.multiple_of(p * 4 * UTT + c * RC, RC), RC), :],
            xin.at[m, pl.ds(pl.multiple_of(c * RC, RC), RC), :],
            f_s.at[c, i], f_r.at[c, i], d, p,
        )

    for c in range(NCH):
        for i in range(1, N_MP):
            feature(c, i).start()

    def number_slots():
        target = dest[...]
        row = lax.bitwise_and(target, FRM - 1)
        shifted = lambda by, top: lax.bitwise_and(lax.shift_right_logical(target, by), top)
        owner = (
            lax.bitwise_and(shifted(14, 3) - z, 3) * 8
            + lax.bitwise_and(shifted(12, 3) - y, 3) * 2
            + lax.bitwise_and(shifted(11, 1) + core, 1)
        )
        before = jnp.where(iota((256, 256), 0) < iota((256, 256), 1), 1.0, 0.0).astype(BF16)
        carry = jnp.zeros((N_DP, 1), F32)
        ranks = []
        for b in range(FRM // 256):
            mine = owner[:, b * 256 : (b + 1) * 256] == iota((N_DP, 256), 0)
            ones = jnp.where(mine, 1.0, 0.0)
            earlier = dot(ones.astype(BF16), before) + carry
            ranks.append(jnp.sum(jnp.where(mine, earlier, 0.0), axis=0, keepdims=True))
            carry = carry + jnp.sum(ones, axis=1, keepdims=True)
        rank = jnp.concatenate(ranks, axis=1).astype(jnp.int32)
        quad[...] = jnp.where(lax.shift_right_logical(owner, 2) == iota((8, FRM), 0), rank, 4096)
        remainder = jnp.where(lax.bitwise_and(owner, 3) == iota((8, FRM), 0), 1.0, 0.0).astype(BF16)
        spread = jnp.where(iota((8, 4 * CH), 0) == lax.div(iota((8, 4 * CH), 1), CH), 1.0, 0.0).astype(BF16)
        for b in range(FRM // 256):
            part_ = slice(b * 256, (b + 1) * 256)
            keep = dot(remainder[:, part_], spread, ((0,), (0,))).astype(BF16)
            rows = grads[part_, :]
            rhs[part_, :] = keep * jnp.concatenate([rows] * 4, axis=1)
        line = iota((2 * N_DP, FRM), 0)
        digits = jnp.where(
            line == owner, lax.shift_right_logical(row, 8),
            jnp.where(line == owner + N_DP, lax.bitwise_and(row, 255), 0),
        ).astype(F32).astype(BF16)
        for odd in range(2):
            pick = jnp.where(iota((256, FRM), 0) == rank + 64 * odd, 1.0, 0.0).astype(BF16)
            meta[odd] = dot(digits, pick, ((1,), (1,)))

    number_slots()

    def routed(k):
        return remote(
            obox.at[k], arrived.at[k], rt_s.at[k], rt_r.at[k],
            dp_of(lax.div(k, 8), lax.rem(lax.div(k, 2), 4), lax.rem(k, 2)), m,
        )

    own_block = pltpu.make_async_copy(obox.at[0], arrived.at[0], rt_r.at[0])

    def pack(g):
        pick = jnp.where(iota((CAP, FRM), 0) == quad[pl.ds(g, 1), :], 1.0, 0.0).astype(BF16)
        both = dot(pick, rhs[...])
        line = iota((META, 128), 0)
        for j in range(4):
            k = g * 4 + j
            obox[k, 0:CAP, :] = both[:, j * CH : (j + 1) * CH].astype(BF16)
            high, low = meta[j % 2, pl.ds(k, 1), :], meta[j % 2, pl.ds(k + N_DP, 1), :]
            tile = jnp.where(line == 0, high[:, :128], jnp.where(line == 1, high[:, 128:], 0.0))
            tile = jnp.where(line == 2, low[:, :128], jnp.where(line == 3, low[:, 128:], tile))
            obox[k, CAP:BLK, :] = tile.astype(BF16)

    @pl.loop(0, 8)
    def _(i):
        g = lax.rem(5 * i + 2, 8)
        pack(g)
        for j in range(1, 4):
            routed(g * 4 + j).start()

        @pl.when(g != 0)
        def _():
            routed(g * 4).start()

        @pl.when(g == 0)
        def _():
            own_block.start()

    for i in range(1, N_MP):
        for w in range(2):
            wx(i, w).wait()

    def along_z(i):
        return dp_of(i, 0, 0)

    def along_y(i):
        return dp_of(0, i, 0)

    def wa(w, i):
        block = wts.at[w, z, y, core]
        return remote(block, block, wa_s.at[w, i], wa_r.at[w, i], (along_z, along_y)[w](i), m)

    def wb(w, i):
        block = wts.at[0, :, y, core] if w == 0 else wts.at[1, z, :, core]
        return remote(block, block, wb_s.at[w, i], wb_r.at[w, i], (along_y, along_z)[w](i), m)

    def wc(w):
        block = wts.at[w, :, :, core]
        return remote(block, block, wc_s.at[w], wc_r.at[w], dp_of(0, 0, 1), m)

    for w in range(2):
        for i in range(1, 4):
            wa(w, i).start()

    def place(g):
        first, second = [], []
        for i in range(4):
            digits = arrived[g * 4 + i, CAP:BLK, :].astype(F32)
            first.append(digits[0:1] * 256.0 + digits[2:3])
            second.append(digits[1:2] * 256.0 + digits[3:4])
        left = iota((1, 128), 1) < 64
        at = jnp.concatenate(
            [
                first[0], jnp.where(left, second[0], first[1]), second[1],
                first[2], jnp.where(left, second[2], first[3]), second[3],
            ],
            axis=1,
        ).astype(jnp.int32)
        half = lax.shift_right_logical(at, 10)
        within = lax.bitwise_and(at, 1023)
        top = jnp.where(iota((8, 4 * CAP), 0) == 0, half, 0).astype(F32).astype(BF16)
        later = dot(top, jnp.ones((8, CH), BF16), ((0,), (0,))).astype(BF16)
        block = arrived[pl.ds(g * 4, 4), 0:CAP, :].reshape(4 * CAP, CH)
        second_half = block * later
        sides = jnp.concatenate([block - second_half, second_half], axis=1)
        for a in range(2):
            pick = jnp.where(iota((UTT, 4 * CAP), 0) + a * UTT == within, 1.0, 0.0).astype(BF16)
            placed[a] += dot(pick, sides)

    placed[...] = jnp.zeros((2, UTT, 2 * CH), F32)
    for w in range(2):
        for i in range(1, 4):
            wa(w, i).wait()
    for w in range(2):
        for i in range(1, 4):
            wb(w, i).start()

    @pl.loop(0, 8)
    def _(i):
        g = lax.rem(5 * i + 2, 8)
        for j in range(1, 4):
            routed(g * 4 + j).wait()

        @pl.when(g != 0)
        def _():
            routed(g * 4).wait()

        @pl.when(g == 0)
        def _():
            own_block.wait()

        place(g)

    def exchange(i):
        p = lax.rem(m + i, N_MP)
        return remote(exb.at[p], mg.at[m], ex_s.at[i], ex_r.at[i], d, p)

    for p in range(N_MP):
        exb[p] = placed[p % 2, :, (p // 2) * CH : (p // 2 + 1) * CH].astype(BF16)
    for i in range(1, N_MP):
        exchange(i).start()
    mg[m] = exb[m]

    for w in range(2):
        for i in range(1, 4):
            wb(w, i).wait()
        wc(w).start()
    own_rows.wait()

    def unpair(c):
        rows = pl.ds(pl.multiple_of(c * RC, RC), RC)
        for g in range(N_MP):
            s32[g] = xin[g, rows, :].astype(F32)
        for j in range(4):
            for g in range(N_MP):
                lanes = slice((j % 2) * C + g * CH, (j % 2) * C + (g + 1) * CH)
                pairs6[c, (j // 2) * FC : (j // 2 + 1) * FC, lanes] = s32[g, pl.ds(j, FC, stride=4), :].astype(BF16)

    def forward(c):
        pre = dot(pairs6[c], wts[0].reshape(2 * C, C))
        half = 0.5 * (1.0 + lax.erf(pre * inv_root_two))
        act = (pre * half).astype(BF16)
        slope6[c] = half + pre * jnp.exp(-0.5 * pre * pre) * inv_root_tau
        pairs7[c, :, 0:C] = act[:FC]
        pairs7[c, :, C : 2 * C] = act[FC:]
        pre = dot(pairs7[c], wts[1].reshape(2 * C, C))
        half = 0.5 * (1.0 + lax.erf(pre * inv_root_two))
        slope7[c] = half + pre * jnp.exp(-0.5 * pre * pre) * inv_root_tau

    @pl.loop(0, NCH)
    def _(c):
        for i in range(1, N_MP):
            feature(c, i).wait()
        unpair(c)

    for w in range(2):
        wc(w).wait()

    @pl.loop(0, NCH)
    def _(c):
        forward(c)

    for i in range(1, N_MP):
        exchange(i).wait()

    valid = lax.div(lens[m] - 400, 320) + 1

    def given(c, i):
        p = lax.rem(m + i, N_MP)
        return remote(
            gout.at[p, pl.ds(pl.multiple_of(c * RC, RC), RC), :],
            gf.at[pl.ds(pl.multiple_of(m * 4 * UTT + c * RC, RC), RC), :],
            go_s.at[c, i], go_r.at[c, i], d, p,
        )

    def own_given(c):
        return pltpu.make_async_copy(
            gout.at[m, pl.ds(pl.multiple_of(c * RC, RC), RC), :],
            gf.at[pl.ds(pl.multiple_of(m * 4 * UTT + c * RC, RC), RC), :],
            go_s.at[c, 0],
        )

    def backward(c):
        frames = pl.ds(pl.multiple_of(c * FC, FC), FC)
        live = iota((FC, CH), 0) + c * FC < valid
        for g in range(N_MP):
            lanes = slice(g * CH, (g + 1) * CH)
            coming = jnp.where(live, mg[g, frames, :].astype(F32), 0.0)
            delta7[c, :, lanes] = (coming * slope7[c, :, lanes]).astype(BF16)
        back = dot(delta7[c], wts[1].reshape(2 * C, C), ((1,), (1,)))
        delta6[c, 0:FC, :] = (back[:, :C] * slope6[c, 0:FC, :]).astype(BF16)
        delta6[c, FC : 2 * FC, :] = (back[:, C:] * slope6[c, FC : 2 * FC, :]).astype(BF16)
        back = dot(delta6[c], wts[0].reshape(2 * C, C), ((1,), (1,)))
        for j in range(4):
            for g in range(N_MP):
                s32[g, pl.ds(j, FC, stride=4), :] = back[
                    (j // 2) * FC : (j // 2 + 1) * FC, (j % 2) * C + g * CH : (j % 2) * C + (g + 1) * CH
                ]
        for g in range(N_MP):
            gout[g, pl.ds(pl.multiple_of(c * RC, RC), RC), :] = s32[g].astype(BF16)

    @pl.loop(0, NCH)
    def _(c):
        backward(c)
        for i in range(1, N_MP):
            given(c, i).start()
        own_given(c).start()

    def terms(w, b):
        pairs, deltas, count = ((pairs6, delta6, 2 * UTT), (pairs7, delta7, UTT))[w]
        left = pairs[:, :, pl.ds(pl.multiple_of(b * 256, 256), 256)].reshape(count, 256)
        right = deltas[...].reshape(count, C)
        gsum[w, b] = dot(left, right, ((0,), (0,))).reshape(4, 2, KR, C)

    def to_mate(w):
        return remote(core_out.at[w], core_in.at[w], rc_s.at[w], rc_r.at[w], dp_of(0, 0, 1), m)

    def ra(w, i):
        p = lax.rem((z, y)[w] + i, 4)
        return remote(
            part_out.at[w, p], part_in.at[w, i], ra_s.at[w, i], ra_r.at[w, i], (along_z, along_y)[w](i), m
        )

    def rb(w, i):
        p = lax.rem((y, z)[w] + i, 4)
        return remote(
            chip_out.at[w, p], chip_in.at[w, i], rb_s.at[w, i], rb_r.at[w, i], (along_y, along_z)[w](i), m
        )

    for w in (1, 0):

        @pl.loop(0, 4)
        def _(b):
            terms(w, b)
            core_out[w, b] = gsum[w, b, :, 1 - core].astype(BF16)

        to_mate(w).start()

    for w in (1, 0):
        to_mate(w).wait()

        @pl.loop(0, 4)
        def _(a):
            for b in range(4):
                zy = (a, b) if w == 0 else (b, a)
                total = gsum[w, zy[0], zy[1], core] + core_in[w, zy[0], zy[1]].astype(F32)
                part_out[w, a, b] = total.astype(BF16)

        for i in range(1, 4):
            ra(w, i).start()

    for w in (1, 0):
        for b in range(4):
            zy = (z, b) if w == 0 else (b, y)
            part[w, b] = gsum[w, zy[0], zy[1], core] + core_in[w, zy[0], zy[1]].astype(F32)
        for i in range(1, 4):
            ra(w, i).wait()
            part[w] += part_in[w, i].astype(F32)
        chip_out[w] = part[w].astype(BF16)
        for i in range(1, 4):
            rb(w, i).start()

    for w in (1, 0):
        share[w] = part[w, (y, z)[w]]
        for i in range(1, 4):
            rb(w, i).wait()
            share[w] += chip_in[w, i].astype(F32)
    for g in range(N_MP):
        x_out[g] = share[:, :, g * CH : (g + 1) * CH]

    def along(i):
        p = lax.rem(m + i, N_MP)
        return remote(x_out.at[p], x_in.at[i], rx_s.at[i], rx_r.at[i], d, p)

    for i in range(1, N_MP):
        along(i).start()
    total = x_out[m]
    for i in range(1, N_MP):
        along(i).wait()
        total = total + x_in[i]
    g6[...] = total[0]
    g7[...] = total[1]

    @pl.loop(0, NCH)
    def _(c):
        for i in range(1, N_MP):
            given(c, i).wait()
        own_given(c).wait()


def body(features, conv6_weight, conv7_weight, frame_grads, frame_dest, lengths):
    d = lax.axis_index("dp")
    own = lax.dynamic_slice_in_dim(frame_dest, d * FRM, FRM, 0).reshape(1, FRM)
    vmem, hbm = pl.BlockSpec(memory_space=pltpu.VMEM), pl.BlockSpec(memory_space=pl.ANY)
    dma = pltpu.SemaphoreType.DMA
    return pl.pallas_call(
        kernel,
        out_shape=(
            jax.ShapeDtypeStruct(features.shape, BF16),
            jax.ShapeDtypeStruct(conv6_weight.shape, F32),
            jax.ShapeDtypeStruct(conv7_weight.shape, F32),
        ),
        in_specs=[hbm, vmem, vmem, vmem, vmem, pl.BlockSpec(memory_space=pltpu.SMEM)],
        out_specs=(hbm, vmem, vmem),
        scratch_shapes=[
            pltpu.VMEM((N_MP, 4 * UTT, CH), BF16),
            pltpu.VMEM((2, 4, 4, 2, KR, C), BF16),
            pltpu.VMEM((8, FRM), jnp.int32),
            pltpu.VMEM((2, 2 * N_DP, 256), F32),
            pltpu.VMEM((FRM, 4 * CH), BF16),
            pltpu.VMEM((N_DP, BLK, CH), BF16),
            pltpu.VMEM((N_DP, BLK, CH), BF16),
            pltpu.VMEM((2, UTT, 2 * CH), F32),
            pltpu.VMEM((N_MP, UTT, CH), BF16),
            pltpu.VMEM((N_MP, UTT, CH), BF16),
            pltpu.VMEM((N_MP, RC, CH), F32),
            pltpu.VMEM((NCH, 2 * FC, 2 * C), BF16),
            pltpu.VMEM((NCH, FC, 2 * C), BF16),
            pltpu.VMEM((NCH, 2 * FC, C), F32),
            pltpu.VMEM((NCH, FC, C), F32),
            pltpu.VMEM((NCH, FC, C), BF16),
            pltpu.VMEM((NCH, 2 * FC, C), BF16),
            pltpu.VMEM((N_MP, 4 * UTT, CH), BF16),
            pltpu.VMEM((2, 4, 4, 2, KR, C), F32),
            pltpu.VMEM((2, 4, 4, KR, C), BF16),
            pltpu.VMEM((2, 4, 4, KR, C), BF16),
            pltpu.VMEM((2, 4, 4, KR, C), BF16),
            pltpu.VMEM((2, 4, 4, KR, C), BF16),
            pltpu.VMEM((2, 4, KR, C), F32),
            pltpu.VMEM((2, 4, KR, C), BF16),
            pltpu.VMEM((2, 4, KR, C), BF16),
            pltpu.VMEM((2, KR, C), F32),
            pltpu.VMEM((N_MP, 2, KR, CH), F32),
            pltpu.VMEM((N_MP, 2, KR, CH), F32),
            dma((N_MP, 2)), dma((N_MP, 2)), dma((2, 4)), dma((2, 4)), dma((2, 4)), dma((2, 4)), dma((2,)), dma((2,)),
            dma((1,)), dma((NCH, N_MP)), dma((NCH, N_MP)), dma((N_DP,)), dma((N_DP,)), dma((N_MP,)), dma((N_MP,)),
            dma((NCH, N_MP)), dma((NCH, N_MP)), dma((2,)), dma((2,)), dma((2, 4)), dma((2, 4)), dma((2, 4)), dma((2, 4)),
            dma((N_MP,)), dma((N_MP,)),
        ],
        compiler_params=pltpu.CompilerParams(
            collective_id=0, has_side_effects=True, vmem_limit_bytes=56 * 2**20,
            fuse_transposed_lhs_in_matmul=True,
        ),
        name="encoder_backward",
    )(features, conv6_weight, conv7_weight, frame_grads, own, lengths)


def solution(mesh):
    placed = (P("dp", "mp"), P("dp", "mp"), P("dp", "mp"), P("dp", "mp"), P(), P("dp"))
    return jax.shard_map(
        body,
        mesh=mesh,
        in_specs=placed,
        out_specs=(P("dp", "mp"), P("dp", "mp"), P("dp", "mp")),
        check_vma=False,
    )
```

```python
import jax
import jax.numpy as jnp
from jax import lax
from jax.experimental import pallas as pl
from jax.experimental.pallas import tpu as pltpu
from jax.sharding import PartitionSpec as P

C = 512
FRM = 2048
CAP = 192
N_DP = 32
N_MP = 4
CH = C // N_MP
UTT = FRM // N_MP
FC = 128
NCH = UTT // FC
RC = 4 * FC
META = 16
BLK = CAP + META
KR = 32

inv_root_two = 0.7071067811865476
inv_root_tau = 0.3989422804014327
F32 = jnp.float32
BF16 = jnp.bfloat16


def dot(left, right, contract=((1,), (0,))):
    return lax.dot_general(left, right, (contract, ((), ())), preferred_element_type=F32)


def iota(shape, axis):
    return lax.broadcasted_iota(jnp.int32, shape, axis)


def kernel(
    feat, w6, w7, grads_in, dest_in, lens_in,
    gf, g6, g7,
    grads, dest, lens, xin, wts, quad, meta, rhs, obox, arrived, placed, exb, mg,
    s32, pairs6, pairs7, slope6, slope7, delta7, delta6, gout,
    gsum, core_out, core_in, part_out, part_in, part, chip_out, chip_in, share, x_out, x_in,
    wa_s, wa_r, wb_s, wb_r, wx_s, wx_r, wc_s, wc_r, own_sem, f_s, f_r, rt_s, rt_r, ex_s, ex_r,
    go_s, go_r, rc_s, rc_r, ra_s, ra_r, rb_s, rb_r, rx_s, rx_r,
):
    d, m = lax.axis_index("dp"), lax.axis_index("mp")
    z, y, core = lax.div(d, 8), lax.rem(lax.div(d, 2), 4), lax.rem(d, 2)

    def dp_of(dz, dy, dc):
        return lax.rem(z + dz, 4) * 8 + lax.rem(y + dy, 4) * 2 + lax.rem(core + dc, 2)

    def remote(src, dst, send, recv, dp, mp):
        return pltpu.make_async_remote_copy(
            src_ref=src, dst_ref=dst, send_sem=send, recv_sem=recv,
            device_id=(dp, mp), device_id_type=pl.DeviceIdType.MESH,
        )

    barrier = pltpu.get_barrier_semaphore()
    for i in range(1, N_MP):
        pl.semaphore_signal(barrier, inc=1, device_id=(d, lax.rem(m + i, N_MP)), device_id_type=pl.DeviceIdType.MESH)

    @pl.loop(1, N_DP)
    def _(k):
        pl.semaphore_signal(barrier, inc=1, device_id=(lax.rem(d + k, N_DP), m), device_id_type=pl.DeviceIdType.MESH)

    own_rows = pltpu.make_async_copy(
        feat.at[pl.ds(pl.multiple_of(m * 4 * UTT, 4 * UTT), 4 * UTT), :], xin.at[m], own_sem.at[0]
    )
    own_rows.start()
    cols = pl.ds(pl.multiple_of(m * CH, CH), CH)
    local = [
        pltpu.make_async_copy(dest_in.at[pl.ds(pl.multiple_of(d * FRM, FRM), FRM)], dest, own_sem.at[1]),
        pltpu.make_async_copy(grads_in, grads, own_sem.at[2]),
        pltpu.make_async_copy(w6, wts.at[0, z, y, core, :, cols], own_sem.at[3]),
        pltpu.make_async_copy(w7, wts.at[1, z, y, core, :, cols], own_sem.at[4]),
        pltpu.make_async_copy(lens_in, lens, own_sem.at[5]),
    ]
    for copy in local:
        copy.start()
    for copy in local:
        copy.wait()
    pl.semaphore_wait(barrier, N_DP - 1 + N_MP - 1)

    def along_z(i):
        return dp_of(i, 0, 0)

    def along_y(i):
        return dp_of(0, i, 0)

    def wa(w, i):
        block = wts.at[w, z, y, core, :, cols]
        return remote(block, block, wa_s.at[w, i], wa_r.at[w, i], (along_z, along_y)[w](i), m)

    def wb(w, i):
        block = wts.at[0, :, y, core, :, cols] if w == 0 else wts.at[1, z, :, core, :, cols]
        return remote(block, block, wb_s.at[w, i], wb_r.at[w, i], (along_y, along_z)[w](i), m)

    def wx(w, i):
        block = wts.at[w, :, :, core, :, cols]
        return remote(block, block, wx_s.at[w, i], wx_r.at[w, i], d, lax.rem(m + i, N_MP))

    def wc(w):
        block = wts.at[w, :, :, core]
        return remote(block, block, wc_s.at[w], wc_r.at[w], dp_of(0, 0, 1), m)

    for w in range(2):
        for i in range(1, 4):
            wa(w, i).start()

    def feature(c, i):
        p = lax.rem(m + i, N_MP)
        return remote(
            feat.at[pl.ds(pl.multiple_of(p * 4 * UTT + c * RC, RC), RC), :],
            xin.at[m, pl.ds(pl.multiple_of(c * RC, RC), RC), :],
            f_s.at[c, i], f_r.at[c, i], d, p,
        )

    for c in range(NCH // 2):
        for i in range(1, N_MP):
            feature(c, i).start()

    def number_slots():
        target = dest[...].reshape(1, FRM)
        row = lax.bitwise_and(target, FRM - 1)
        shifted = lambda by, top: lax.bitwise_and(lax.shift_right_logical(target, by), top)
        owner = (
            lax.bitwise_and(shifted(14, 3) - z, 3) * 8
            + lax.bitwise_and(shifted(12, 3) - y, 3) * 2
            + lax.bitwise_and(shifted(11, 1) + core, 1)
        )
        before = jnp.where(iota((256, 256), 0) < iota((256, 256), 1), 1.0, 0.0).astype(BF16)
        carry = jnp.zeros((N_DP, 1), F32)
        ranks = []
        for b in range(FRM // 256):
            mine = owner[:, b * 256 : (b + 1) * 256] == iota((N_DP, 256), 0)
            ones = jnp.where(mine, 1.0, 0.0)
            earlier = dot(ones.astype(BF16), before) + carry
            ranks.append(jnp.sum(jnp.where(mine, earlier, 0.0), axis=0, keepdims=True))
            carry = carry + jnp.sum(ones, axis=1, keepdims=True)
        rank = jnp.concatenate(ranks, axis=1).astype(jnp.int32)
        quad[...] = jnp.where(lax.shift_right_logical(owner, 2) == iota((8, FRM), 0), rank, 4096)
        remainder = jnp.where(lax.bitwise_and(owner, 3) == iota((8, FRM), 0), 1.0, 0.0).astype(BF16)
        spread = jnp.where(iota((8, 4 * CH), 0) == lax.div(iota((8, 4 * CH), 1), CH), 1.0, 0.0).astype(BF16)
        for b in range(FRM // 256):
            part_ = slice(b * 256, (b + 1) * 256)
            keep = dot(remainder[:, part_], spread, ((0,), (0,))).astype(BF16)
            rows = grads[part_, :]
            rhs[part_, :] = keep * jnp.concatenate([rows] * 4, axis=1)
        line = iota((2 * N_DP, FRM), 0)
        digits = jnp.where(
            line == owner, lax.shift_right_logical(row, 8),
            jnp.where(line == owner + N_DP, lax.bitwise_and(row, 255), 0),
        ).astype(F32).astype(BF16)
        for odd in range(2):
            pick = jnp.where(iota((256, FRM), 0) == rank + 64 * odd, 1.0, 0.0).astype(BF16)
            meta[odd] = dot(digits, pick, ((1,), (1,)))

    number_slots()
    for w in range(2):
        for i in range(1, 4):
            wa(w, i).wait()
    for w in range(2):
        for i in range(1, 4):
            wb(w, i).start()

    def routed(k):
        return remote(
            obox.at[k], arrived.at[k], rt_s.at[k], rt_r.at[k],
            dp_of(lax.div(k, 8), lax.rem(lax.div(k, 2), 4), lax.rem(k, 2)), m,
        )

    own_block = pltpu.make_async_copy(obox.at[0], arrived.at[0], rt_r.at[0])

    def pack(g):
        pick = jnp.where(iota((CAP, FRM), 0) == quad[pl.ds(g, 1), :], 1.0, 0.0).astype(BF16)
        both = dot(pick, rhs[...])
        line = iota((META, 128), 0)
        for j in range(4):
            k = g * 4 + j
            obox[k, 0:CAP, :] = both[:, j * CH : (j + 1) * CH].astype(BF16)
            high, low = meta[j % 2, pl.ds(k, 1), :], meta[j % 2, pl.ds(k + N_DP, 1), :]
            tile = jnp.where(line == 0, high[:, :128], jnp.where(line == 1, high[:, 128:], 0.0))
            tile = jnp.where(line == 2, low[:, :128], jnp.where(line == 3, low[:, 128:], tile))
            obox[k, CAP:BLK, :] = tile.astype(BF16)

    @pl.loop(0, 8)
    def _(i):
        g = lax.rem(5 * i + 2, 8)
        pack(g)
        for j in range(1, 4):
            routed(g * 4 + j).start()

        @pl.when(g != 0)
        def _():
            routed(g * 4).start()

        @pl.when(g == 0)
        def _():
            own_block.start()

    for w in range(2):
        for i in range(1, 4):
            wb(w, i).wait()
    for w in range(2):
        for i in range(1, 4):
            wx(w, i).start()
    for c in range(NCH // 2, NCH):
        for i in range(1, N_MP):
            feature(c, i).start()

    def place(g):
        first, second = [], []
        for i in range(4):
            digits = arrived[g * 4 + i, CAP:BLK, :].astype(F32)
            first.append(digits[0:1] * 256.0 + digits[2:3])
            second.append(digits[1:2] * 256.0 + digits[3:4])
        left = iota((1, 128), 1) < 64
        at = jnp.concatenate(
            [
                first[0], jnp.where(left, second[0], first[1]), second[1],
                first[2], jnp.where(left, second[2], first[3]), second[3],
            ],
            axis=1,
        ).astype(jnp.int32)
        half = lax.shift_right_logical(at, 10)
        within = lax.bitwise_and(at, 1023)
        top = jnp.where(iota((8, 4 * CAP), 0) == 0, half, 0).astype(F32).astype(BF16)
        later = dot(top, jnp.ones((8, CH), BF16), ((0,), (0,))).astype(BF16)
        block = arrived[pl.ds(g * 4, 4), 0:CAP, :].reshape(4 * CAP, CH)
        second_half = block * later
        sides = jnp.concatenate([block - second_half, second_half], axis=1)
        for a in range(2):
            pick = jnp.where(iota((UTT, 4 * CAP), 0) + a * UTT == within, 1.0, 0.0).astype(BF16)
            placed[a] += dot(pick, sides)

    placed[...] = jnp.zeros((2, UTT, 2 * CH), F32)

    @pl.loop(0, 8)
    def _(i):
        g = lax.rem(5 * i + 2, 8)
        for j in range(1, 4):
            routed(g * 4 + j).wait()

        @pl.when(g != 0)
        def _():
            routed(g * 4).wait()

        @pl.when(g == 0)
        def _():
            own_block.wait()

        place(g)

    def exchange(i):
        p = lax.rem(m + i, N_MP)
        return remote(exb.at[p], mg.at[m], ex_s.at[i], ex_r.at[i], d, p)

    for p in range(N_MP):
        exb[p] = placed[p % 2, :, (p // 2) * CH : (p // 2 + 1) * CH].astype(BF16)
    for i in range(1, N_MP):
        exchange(i).start()
    mg[m] = exb[m]

    for w in range(2):
        for i in range(1, 4):
            wx(w, i).wait()
        wc(w).start()
    own_rows.wait()

    def unpair(c):
        rows = pl.ds(pl.multiple_of(c * RC, RC), RC)
        for g in range(N_MP):
            s32[g] = xin[g, rows, :].astype(F32)
        for j in range(4):
            for g in range(N_MP):
                lanes = slice((j % 2) * C + g * CH, (j % 2) * C + (g + 1) * CH)
                pairs6[c, (j // 2) * FC : (j // 2 + 1) * FC, lanes] = s32[g, pl.ds(j, FC, stride=4), :].astype(BF16)

    def forward(c):
        pre = dot(pairs6[c], wts[0].reshape(2 * C, C))
        half = 0.5 * (1.0 + lax.erf(pre * inv_root_two))
        act = (pre * half).astype(BF16)
        slope6[c] = half + pre * jnp.exp(-0.5 * pre * pre) * inv_root_tau
        pairs7[c, :, 0:C] = act[:FC]
        pairs7[c, :, C : 2 * C] = act[FC:]
        pre = dot(pairs7[c], wts[1].reshape(2 * C, C))
        half = 0.5 * (1.0 + lax.erf(pre * inv_root_two))
        slope7[c] = half + pre * jnp.exp(-0.5 * pre * pre) * inv_root_tau

    @pl.loop(0, NCH)
    def _(c):
        for i in range(1, N_MP):
            feature(c, i).wait()
        unpair(c)

    for w in range(2):
        wc(w).wait()

    @pl.loop(0, NCH)
    def _(c):
        forward(c)

    for i in range(1, N_MP):
        exchange(i).wait()

    valid = lax.div(lens[m] - 400, 320) + 1

    def given(c, i):
        p = lax.rem(m + i, N_MP)
        return remote(
            gout.at[p, pl.ds(pl.multiple_of(c * RC, RC), RC), :],
            gf.at[pl.ds(pl.multiple_of(m * 4 * UTT + c * RC, RC), RC), :],
            go_s.at[c, i], go_r.at[c, i], d, p,
        )

    def own_given(c):
        return pltpu.make_async_copy(
            gout.at[m, pl.ds(pl.multiple_of(c * RC, RC), RC), :],
            gf.at[pl.ds(pl.multiple_of(m * 4 * UTT + c * RC, RC), RC), :],
            go_s.at[c, 0],
        )

    def backward(c):
        frames = pl.ds(pl.multiple_of(c * FC, FC), FC)
        live = iota((FC, CH), 0) + c * FC < valid
        for g in range(N_MP):
            lanes = slice(g * CH, (g + 1) * CH)
            coming = jnp.where(live, mg[g, frames, :].astype(F32), 0.0)
            delta7[c, :, lanes] = (coming * slope7[c, :, lanes]).astype(BF16)
        back = dot(delta7[c], wts[1].reshape(2 * C, C), ((1,), (1,)))
        delta6[c, 0:FC, :] = (back[:, :C] * slope6[c, 0:FC, :]).astype(BF16)
        delta6[c, FC : 2 * FC, :] = (back[:, C:] * slope6[c, FC : 2 * FC, :]).astype(BF16)
        back = dot(delta6[c], wts[0].reshape(2 * C, C), ((1,), (1,)))
        for j in range(4):
            for g in range(N_MP):
                s32[g, pl.ds(j, FC, stride=4), :] = back[
                    (j // 2) * FC : (j // 2 + 1) * FC, (j % 2) * C + g * CH : (j % 2) * C + (g + 1) * CH
                ]
        for g in range(N_MP):
            gout[g, pl.ds(pl.multiple_of(c * RC, RC), RC), :] = s32[g].astype(BF16)

    @pl.loop(0, NCH)
    def _(c):
        backward(c)
        for i in range(1, N_MP):
            given(c, i).start()
        own_given(c).start()

    def terms(w, b):
        pairs, deltas, count = ((pairs6, delta6, 2 * UTT), (pairs7, delta7, UTT))[w]
        left = pairs[:, :, pl.ds(pl.multiple_of(b * 256, 256), 256)].reshape(count, 256)
        right = deltas[...].reshape(count, C)
        gsum[w, b] = dot(left, right, ((0,), (0,))).reshape(4, 2, KR, C)

    def to_mate(w):
        return remote(core_out.at[w], core_in.at[w], rc_s.at[w], rc_r.at[w], dp_of(0, 0, 1), m)

    def ra(w, i):
        p = lax.rem((z, y)[w] + i, 4)
        return remote(
            part_out.at[w, p], part_in.at[w, i], ra_s.at[w, i], ra_r.at[w, i], (along_z, along_y)[w](i), m
        )

    def rb(w, i):
        p = lax.rem((y, z)[w] + i, 4)
        return remote(
            chip_out.at[w, p], chip_in.at[w, i], rb_s.at[w, i], rb_r.at[w, i], (along_y, along_z)[w](i), m
        )

    for w in (1, 0):

        @pl.loop(0, 4)
        def _(b):
            terms(w, b)
            core_out[w, b] = gsum[w, b, :, 1 - core].astype(BF16)

        to_mate(w).start()

    for w in (1, 0):
        to_mate(w).wait()

        @pl.loop(0, 4)
        def _(a):
            for b in range(4):
                zy = (a, b) if w == 0 else (b, a)
                total = gsum[w, zy[0], zy[1], core] + core_in[w, zy[0], zy[1]].astype(F32)
                part_out[w, a, b] = total.astype(BF16)

        for i in range(1, 4):
            ra(w, i).start()

    for w in (1, 0):
        for b in range(4):
            zy = (z, b) if w == 0 else (b, y)
            part[w, b] = gsum[w, zy[0], zy[1], core] + core_in[w, zy[0], zy[1]].astype(F32)
        for i in range(1, 4):
            ra(w, i).wait()
            part[w] += part_in[w, i].astype(F32)
        chip_out[w] = part[w].astype(BF16)
        for i in range(1, 4):
            rb(w, i).start()

    for w in (1, 0):
        share[w] = part[w, (y, z)[w]]
        for i in range(1, 4):
            rb(w, i).wait()
            share[w] += chip_in[w, i].astype(F32)
    for g in range(N_MP):
        x_out[g] = share[:, :, g * CH : (g + 1) * CH]

    def along(i):
        p = lax.rem(m + i, N_MP)
        return remote(x_out.at[p], x_in.at[i], rx_s.at[i], rx_r.at[i], d, p)

    for i in range(1, N_MP):
        along(i).start()
    total = x_out[m]
    for i in range(1, N_MP):
        along(i).wait()
        total = total + x_in[i]
    g6[...] = total[0]
    g7[...] = total[1]

    @pl.loop(0, NCH)
    def _(c):
        for i in range(1, N_MP):
            given(c, i).wait()
        own_given(c).wait()


def body(features, conv6_weight, conv7_weight, frame_grads, frame_dest, lengths):
    vmem, hbm = pl.BlockSpec(memory_space=pltpu.VMEM), pl.BlockSpec(memory_space=pl.ANY)
    dma = pltpu.SemaphoreType.DMA
    return pl.pallas_call(
        kernel,
        out_shape=(
            jax.ShapeDtypeStruct(features.shape, BF16),
            jax.ShapeDtypeStruct(conv6_weight.shape, F32),
            jax.ShapeDtypeStruct(conv7_weight.shape, F32),
        ),
        in_specs=[hbm] * 6,
        out_specs=(hbm, vmem, vmem),
        scratch_shapes=[
            pltpu.VMEM((FRM, CH), BF16),
            pltpu.VMEM((FRM,), jnp.int32),
            pltpu.SMEM((N_MP,), jnp.int32),
            pltpu.VMEM((N_MP, 4 * UTT, CH), BF16),
            pltpu.VMEM((2, 4, 4, 2, KR, C), BF16),
            pltpu.VMEM((8, FRM), jnp.int32),
            pltpu.VMEM((2, 2 * N_DP, 256), F32),
            pltpu.VMEM((FRM, 4 * CH), BF16),
            pltpu.VMEM((N_DP, BLK, CH), BF16),
            pltpu.VMEM((N_DP, BLK, CH), BF16),
            pltpu.VMEM((2, UTT, 2 * CH), F32),
            pltpu.VMEM((N_MP, UTT, CH), BF16),
            pltpu.VMEM((N_MP, UTT, CH), BF16),
            pltpu.VMEM((N_MP, RC, CH), F32),
            pltpu.VMEM((NCH, 2 * FC, 2 * C), BF16),
            pltpu.VMEM((NCH, FC, 2 * C), BF16),
            pltpu.VMEM((NCH, 2 * FC, C), F32),
            pltpu.VMEM((NCH, FC, C), F32),
            pltpu.VMEM((NCH, FC, C), BF16),
            pltpu.VMEM((NCH, 2 * FC, C), BF16),
            pltpu.VMEM((N_MP, 4 * UTT, CH), BF16),
            pltpu.VMEM((2, 4, 4, 2, KR, C), F32),
            pltpu.VMEM((2, 4, 4, KR, C), BF16),
            pltpu.VMEM((2, 4, 4, KR, C), BF16),
            pltpu.VMEM((2, 4, 4, KR, C), BF16),
            pltpu.VMEM((2, 4, 4, KR, C), BF16),
            pltpu.VMEM((2, 4, KR, C), F32),
            pltpu.VMEM((2, 4, KR, C), BF16),
            pltpu.VMEM((2, 4, KR, C), BF16),
            pltpu.VMEM((2, KR, C), F32),
            pltpu.VMEM((N_MP, 2, KR, CH), F32),
            pltpu.VMEM((N_MP, 2, KR, CH), F32),
            dma((2, 4)), dma((2, 4)), dma((2, 4)), dma((2, 4)), dma((2, 4)), dma((2, 4)), dma((2,)), dma((2,)),
            dma((6,)), dma((NCH, N_MP)), dma((NCH, N_MP)), dma((N_DP,)), dma((N_DP,)), dma((N_MP,)), dma((N_MP,)),
            dma((NCH, N_MP)), dma((NCH, N_MP)), dma((2,)), dma((2,)), dma((2, 4)), dma((2, 4)), dma((2, 4)), dma((2, 4)),
            dma((N_MP,)), dma((N_MP,)),
        ],
        compiler_params=pltpu.CompilerParams(
            collective_id=0, has_side_effects=True, vmem_limit_bytes=56 * 2**20,
            fuse_transposed_lhs_in_matmul=True,
        ),
        name="encoder_backward",
    )(features, conv6_weight, conv7_weight, frame_grads, frame_dest, lengths)


def solution(mesh):
    placed = (P("dp", "mp"), P("dp", "mp"), P("dp", "mp"), P("dp", "mp"), P(), P("dp"))
    return jax.shard_map(
        body,
        mesh=mesh,
        in_specs=placed,
        out_specs=(P("dp", "mp"), P("dp", "mp"), P("dp", "mp")),
        check_vma=False,
    )
```

```python
import jax
import jax.numpy as jnp
from jax import lax
from jax.experimental import pallas as pl
from jax.experimental.pallas import tpu as pltpu
from jax.sharding import PartitionSpec as P

C = 512
FRM = 2048
CAP = 192
N_DP = 32
N_MP = 4
CH = C // N_MP
UTT = FRM // N_MP
FC = 128
NCH = UTT // FC
RC = 4 * FC
META = 16
BLK = CAP + META
KR = 32

inv_root_two = 0.7071067811865476
inv_root_tau = 0.3989422804014327
F32 = jnp.float32
BF16 = jnp.bfloat16


def dot(left, right, contract=((1,), (0,))):
    return lax.dot_general(left, right, (contract, ((), ())), preferred_element_type=F32)


def iota(shape, axis):
    return lax.broadcasted_iota(jnp.int32, shape, axis)


def kernel(
    feat, w6, w7, grads_in, dest_in, lens_in,
    gf, g6, g7,
    grads, dest, lens, xin, wts, quad, meta, rhs, obox, arrived, placed, exb, mg,
    s32, pairs6, pairs7, slope6, slope7, delta7, delta6, gout,
    gsum, core_out, core_in, part_out, part_in, part, chip_out, chip_in, share, x_out, x_in,
    va_s, va_r, vb_s, vb_r, vx_s, vx_r, ux_s, ux_r, ua_s, ua_r, ub_s, ub_r, wc_s, wc_r, own_sem, f_s, f_r, rt_s, rt_r, ex_s, ex_r,
    go_s, go_r, rc_s, rc_r, ra_s, ra_r, rb_s, rb_r, rx_s, rx_r,
):
    d, m = lax.axis_index("dp"), lax.axis_index("mp")
    z, y, core = lax.div(d, 8), lax.rem(lax.div(d, 2), 4), lax.rem(d, 2)

    def dp_of(dz, dy, dc):
        return lax.rem(z + dz, 4) * 8 + lax.rem(y + dy, 4) * 2 + lax.rem(core + dc, 2)

    def remote(src, dst, send, recv, dp, mp):
        return pltpu.make_async_remote_copy(
            src_ref=src, dst_ref=dst, send_sem=send, recv_sem=recv,
            device_id=(dp, mp), device_id_type=pl.DeviceIdType.MESH,
        )

    barrier = pltpu.get_barrier_semaphore()
    for i in range(1, N_MP):
        pl.semaphore_signal(barrier, inc=1, device_id=(d, lax.rem(m + i, N_MP)), device_id_type=pl.DeviceIdType.MESH)

    @pl.loop(1, N_DP)
    def _(k):
        pl.semaphore_signal(barrier, inc=1, device_id=(lax.rem(d + k, N_DP), m), device_id_type=pl.DeviceIdType.MESH)

    own_rows = pltpu.make_async_copy(
        feat.at[pl.ds(pl.multiple_of(m * 4 * UTT, 4 * UTT), 4 * UTT), :], xin.at[m], own_sem.at[0]
    )
    own_rows.start()
    cols = pl.ds(pl.multiple_of(m * CH, CH), CH)
    local = [
        pltpu.make_async_copy(dest_in.at[pl.ds(pl.multiple_of(d * FRM, FRM), FRM)], dest, own_sem.at[1]),
        pltpu.make_async_copy(grads_in, grads, own_sem.at[2]),
        pltpu.make_async_copy(w6, wts.at[0, z, y, core, :, cols], own_sem.at[3]),
        pltpu.make_async_copy(w7, wts.at[1, z, y, core, :, cols], own_sem.at[4]),
        pltpu.make_async_copy(lens_in, lens, own_sem.at[5]),
    ]
    for copy in local:
        copy.start()
    for copy in local:
        copy.wait()
    pl.semaphore_wait(barrier, N_DP - 1 + N_MP - 1)

    def along_z(i):
        return dp_of(i, 0, 0)

    def along_y(i):
        return dp_of(0, i, 0)

    def va(i):
        block = wts.at[1, z, y, core, :, cols]
        return remote(block, block, va_s.at[i], va_r.at[i], along_y(i), m)

    def vb(i):
        block = wts.at[1, z, :, core, :, cols]
        return remote(block, block, vb_s.at[i], vb_r.at[i], along_z(i), m)

    def vx(i):
        block = wts.at[1, :, :, core, :, cols]
        return remote(block, block, vx_s.at[i], vx_r.at[i], d, lax.rem(m + i, N_MP))

    def ux(i):
        block = wts.at[0, z, y, core, :, cols]
        return remote(block, block, ux_s.at[i], ux_r.at[i], d, lax.rem(m + i, N_MP))

    def ua(h, i):
        block = wts.at[0, z, y, core, :, pl.ds(h * 256, 256)]
        return remote(block, block, ua_s.at[h, i], ua_r.at[h, i], (along_z, along_y)[h](i), m)

    def ub(h, i):
        half = pl.ds(h * 256, 256)
        block = wts.at[0, :, y, core, :, half] if h == 0 else wts.at[0, z, :, core, :, half]
        return remote(block, block, ub_s.at[h, i], ub_r.at[h, i], (along_y, along_z)[h](i), m)

    def wc(w):
        block = wts.at[w, :, :, core]
        return remote(block, block, wc_s.at[w], wc_r.at[w], dp_of(0, 0, 1), m)

    for i in range(1, 4):
        ux(i).start()
        va(i).start()

    def feature(c, i):
        p = lax.rem(m + i, N_MP)
        return remote(
            feat.at[pl.ds(pl.multiple_of(p * 4 * UTT + c * RC, RC), RC), :],
            xin.at[m, pl.ds(pl.multiple_of(c * RC, RC), RC), :],
            f_s.at[c, i], f_r.at[c, i], d, p,
        )

    for c in range(NCH // 2):
        for i in range(1, N_MP):
            feature(c, i).start()

    def number_slots():
        target = dest[...].reshape(1, FRM)
        row = lax.bitwise_and(target, FRM - 1)
        shifted = lambda by, top: lax.bitwise_and(lax.shift_right_logical(target, by), top)
        owner = (
            lax.bitwise_and(shifted(14, 3) - z, 3) * 8
            + lax.bitwise_and(shifted(12, 3) - y, 3) * 2
            + lax.bitwise_and(shifted(11, 1) + core, 1)
        )
        before = jnp.where(iota((256, 256), 0) < iota((256, 256), 1), 1.0, 0.0).astype(BF16)
        carry = jnp.zeros((N_DP, 1), F32)
        ranks = []
        for b in range(FRM // 256):
            mine = owner[:, b * 256 : (b + 1) * 256] == iota((N_DP, 256), 0)
            ones = jnp.where(mine, 1.0, 0.0)
            earlier = dot(ones.astype(BF16), before) + carry
            ranks.append(jnp.sum(jnp.where(mine, earlier, 0.0), axis=0, keepdims=True))
            carry = carry + jnp.sum(ones, axis=1, keepdims=True)
        rank = jnp.concatenate(ranks, axis=1).astype(jnp.int32)
        quad[...] = jnp.where(lax.shift_right_logical(owner, 2) == iota((8, FRM), 0), rank, 4096)
        remainder = jnp.where(lax.bitwise_and(owner, 3) == iota((8, FRM), 0), 1.0, 0.0).astype(BF16)
        spread = jnp.where(iota((8, 4 * CH), 0) == lax.div(iota((8, 4 * CH), 1), CH), 1.0, 0.0).astype(BF16)
        for b in range(FRM // 256):
            part_ = slice(b * 256, (b + 1) * 256)
            keep = dot(remainder[:, part_], spread, ((0,), (0,))).astype(BF16)
            rows = grads[part_, :]
            rhs[part_, :] = keep * jnp.concatenate([rows] * 4, axis=1)
        line = iota((2 * N_DP, FRM), 0)
        digits = jnp.where(
            line == owner, lax.shift_right_logical(row, 8),
            jnp.where(line == owner + N_DP, lax.bitwise_and(row, 255), 0),
        ).astype(F32).astype(BF16)
        for odd in range(2):
            pick = jnp.where(iota((256, FRM), 0) == rank + 64 * odd, 1.0, 0.0).astype(BF16)
            meta[odd] = dot(digits, pick, ((1,), (1,)))

    number_slots()
    for i in range(1, 4):
        va(i).wait()
        ux(i).wait()
    for i in range(1, 4):
        vb(i).start()
        ua(0, i).start()
        ua(1, i).start()

    def routed(k):
        return remote(
            obox.at[k], arrived.at[k], rt_s.at[k], rt_r.at[k],
            dp_of(lax.div(k, 8), lax.rem(lax.div(k, 2), 4), lax.rem(k, 2)), m,
        )

    own_block = pltpu.make_async_copy(obox.at[0], arrived.at[0], rt_r.at[0])

    def pack(g):
        pick = jnp.where(iota((CAP, FRM), 0) == quad[pl.ds(g, 1), :], 1.0, 0.0).astype(BF16)
        both = dot(pick, rhs[...])
        line = iota((META, 128), 0)
        for j in range(4):
            k = g * 4 + j
            obox[k, 0:CAP, :] = both[:, j * CH : (j + 1) * CH].astype(BF16)
            high, low = meta[j % 2, pl.ds(k, 1), :], meta[j % 2, pl.ds(k + N_DP, 1), :]
            tile = jnp.where(line == 0, high[:, :128], jnp.where(line == 1, high[:, 128:], 0.0))
            tile = jnp.where(line == 2, low[:, :128], jnp.where(line == 3, low[:, 128:], tile))
            obox[k, CAP:BLK, :] = tile.astype(BF16)

    @pl.loop(0, 8)
    def _(i):
        g = lax.rem(5 * i + 2, 8)
        pack(g)
        for j in range(1, 4):
            routed(g * 4 + j).start()

        @pl.when(g != 0)
        def _():
            routed(g * 4).start()

        @pl.when(g == 0)
        def _():
            own_block.start()

    for i in range(1, 4):
        vb(i).wait()
        ua(0, i).wait()
        ua(1, i).wait()
    for i in range(1, 4):
        vx(i).start()
        ub(0, i).start()
        ub(1, i).start()
    for c in range(NCH // 2, NCH):
        for i in range(1, N_MP):
            feature(c, i).start()

    def place(g):
        first, second = [], []
        for i in range(4):
            digits = arrived[g * 4 + i, CAP:BLK, :].astype(F32)
            first.append(digits[0:1] * 256.0 + digits[2:3])
            second.append(digits[1:2] * 256.0 + digits[3:4])
        left = iota((1, 128), 1) < 64
        at = jnp.concatenate(
            [
                first[0], jnp.where(left, second[0], first[1]), second[1],
                first[2], jnp.where(left, second[2], first[3]), second[3],
            ],
            axis=1,
        ).astype(jnp.int32)
        half = lax.shift_right_logical(at, 10)
        within = lax.bitwise_and(at, 1023)
        top = jnp.where(iota((8, 4 * CAP), 0) == 0, half, 0).astype(F32).astype(BF16)
        later = dot(top, jnp.ones((8, CH), BF16), ((0,), (0,))).astype(BF16)
        block = arrived[pl.ds(g * 4, 4), 0:CAP, :].reshape(4 * CAP, CH)
        second_half = block * later
        sides = jnp.concatenate([block - second_half, second_half], axis=1)
        for a in range(2):
            pick = jnp.where(iota((UTT, 4 * CAP), 0) + a * UTT == within, 1.0, 0.0).astype(BF16)
            placed[a] += dot(pick, sides)

    placed[...] = jnp.zeros((2, UTT, 2 * CH), F32)

    @pl.loop(0, 8)
    def _(i):
        g = lax.rem(5 * i + 2, 8)
        for j in range(1, 4):
            routed(g * 4 + j).wait()

        @pl.when(g != 0)
        def _():
            routed(g * 4).wait()

        @pl.when(g == 0)
        def _():
            own_block.wait()

        place(g)

    def exchange(i):
        p = lax.rem(m + i, N_MP)
        return remote(exb.at[p], mg.at[m], ex_s.at[i], ex_r.at[i], d, p)

    for p in range(N_MP):
        exb[p] = placed[p % 2, :, (p // 2) * CH : (p // 2 + 1) * CH].astype(BF16)
    for i in range(1, N_MP):
        exchange(i).start()
    mg[m] = exb[m]

    for i in range(1, 4):
        ub(0, i).wait()
        ub(1, i).wait()
    wc(0).start()
    for i in range(1, 4):
        vx(i).wait()
    wc(1).start()
    own_rows.wait()

    def unpair(c):
        rows = pl.ds(pl.multiple_of(c * RC, RC), RC)
        for g in range(N_MP):
            s32[g] = xin[g, rows, :].astype(F32)
        for j in range(4):
            for g in range(N_MP):
                lanes = slice((j % 2) * C + g * CH, (j % 2) * C + (g + 1) * CH)
                pairs6[c, (j // 2) * FC : (j // 2 + 1) * FC, lanes] = s32[g, pl.ds(j, FC, stride=4), :].astype(BF16)

    def forward(c):
        pre = dot(pairs6[c], wts[0].reshape(2 * C, C))
        half = 0.5 * (1.0 + lax.erf(pre * inv_root_two))
        act = (pre * half).astype(BF16)
        slope6[c] = half + pre * jnp.exp(-0.5 * pre * pre) * inv_root_tau
        pairs7[c, :, 0:C] = act[:FC]
        pairs7[c, :, C : 2 * C] = act[FC:]
        pre = dot(pairs7[c], wts[1].reshape(2 * C, C))
        half = 0.5 * (1.0 + lax.erf(pre * inv_root_two))
        slope7[c] = half + pre * jnp.exp(-0.5 * pre * pre) * inv_root_tau

    for c in range(2):
        for i in range(1, N_MP):
            feature(c, i).wait()
        unpair(c)
    for w in range(2):
        wc(w).wait()
    for c in range(NCH):
        if c >= 2:
            for i in range(1, N_MP):
                feature(c, i).wait()
            unpair(c)
        forward(c)

    for i in range(1, N_MP):
        exchange(i).wait()

    valid = lax.div(lens[m] - 400, 320) + 1

    def given(c, i):
        p = lax.rem(m + i, N_MP)
        return remote(
            gout.at[p, pl.ds(pl.multiple_of(c * RC, RC), RC), :],
            gf.at[pl.ds(pl.multiple_of(m * 4 * UTT + c * RC, RC), RC), :],
            go_s.at[c, i], go_r.at[c, i], d, p,
        )

    def own_given(c):
        return pltpu.make_async_copy(
            gout.at[m, pl.ds(pl.multiple_of(c * RC, RC), RC), :],
            gf.at[pl.ds(pl.multiple_of(m * 4 * UTT + c * RC, RC), RC), :],
            go_s.at[c, 0],
        )

    def backward(c):
        frames = pl.ds(pl.multiple_of(c * FC, FC), FC)
        live = iota((FC, CH), 0) + c * FC < valid
        for g in range(N_MP):
            lanes = slice(g * CH, (g + 1) * CH)
            coming = jnp.where(live, mg[g, frames, :].astype(F32), 0.0)
            delta7[c, :, lanes] = (coming * slope7[c, :, lanes]).astype(BF16)
        back = dot(delta7[c], wts[1].reshape(2 * C, C), ((1,), (1,)))
        delta6[c, 0:FC, :] = (back[:, :C] * slope6[c, 0:FC, :]).astype(BF16)
        delta6[c, FC : 2 * FC, :] = (back[:, C:] * slope6[c, FC : 2 * FC, :]).astype(BF16)
        back = dot(delta6[c], wts[0].reshape(2 * C, C), ((1,), (1,)))
        for j in range(4):
            for g in range(N_MP):
                s32[g, pl.ds(j, FC, stride=4), :] = back[
                    (j // 2) * FC : (j // 2 + 1) * FC, (j % 2) * C + g * CH : (j % 2) * C + (g + 1) * CH
                ]
        for g in range(N_MP):
            gout[g, pl.ds(pl.multiple_of(c * RC, RC), RC), :] = s32[g].astype(BF16)

    @pl.loop(0, NCH)
    def _(c):
        backward(c)
        for i in range(1, N_MP):
            given(c, i).start()
        own_given(c).start()

    def terms(w, b):
        pairs, deltas, count = ((pairs6, delta6, 2 * UTT), (pairs7, delta7, UTT))[w]
        left = pairs[:, :, pl.ds(pl.multiple_of(b * 256, 256), 256)].reshape(count, 256)
        right = deltas[...].reshape(count, C)
        gsum[w, b] = dot(left, right, ((0,), (0,))).reshape(4, 2, KR, C)

    def to_mate(w):
        return remote(core_out.at[w], core_in.at[w], rc_s.at[w], rc_r.at[w], dp_of(0, 0, 1), m)

    def ra(w, i):
        p = lax.rem((z, y)[w] + i, 4)
        return remote(
            part_out.at[w, p], part_in.at[w, i], ra_s.at[w, i], ra_r.at[w, i], (along_z, along_y)[w](i), m
        )

    def rb(w, i):
        p = lax.rem((y, z)[w] + i, 4)
        return remote(
            chip_out.at[w, p], chip_in.at[w, i], rb_s.at[w, i], rb_r.at[w, i], (along_y, along_z)[w](i), m
        )

    for w in (1, 0):

        @pl.loop(0, 4)
        def _(b):
            terms(w, b)
            core_out[w, b] = gsum[w, b, :, 1 - core].astype(BF16)

        to_mate(w).start()

    for w in (1, 0):
        to_mate(w).wait()

        @pl.loop(0, 4)
        def _(a):
            for b in range(4):
                zy = (a, b) if w == 0 else (b, a)
                total = gsum[w, zy[0], zy[1], core] + core_in[w, zy[0], zy[1]].astype(F32)
                part_out[w, a, b] = total.astype(BF16)

        for i in range(1, 4):
            ra(w, i).start()

    for w in (1, 0):
        for b in range(4):
            zy = (z, b) if w == 0 else (b, y)
            part[w, b] = gsum[w, zy[0], zy[1], core] + core_in[w, zy[0], zy[1]].astype(F32)
        for i in range(1, 4):
            ra(w, i).wait()
            part[w] += part_in[w, i].astype(F32)
        chip_out[w] = part[w].astype(BF16)
        for i in range(1, 4):
            rb(w, i).start()

    for w in (1, 0):
        share[w] = part[w, (y, z)[w]]
        for i in range(1, 4):
            rb(w, i).wait()
            share[w] += chip_in[w, i].astype(F32)
    for g in range(N_MP):
        x_out[g] = share[:, :, g * CH : (g + 1) * CH]

    def along(i):
        p = lax.rem(m + i, N_MP)
        return remote(x_out.at[p], x_in.at[i], rx_s.at[i], rx_r.at[i], d, p)

    for i in range(1, N_MP):
        along(i).start()
    total = x_out[m]
    for i in range(1, N_MP):
        along(i).wait()
        total = total + x_in[i]
    g6[...] = total[0]
    g7[...] = total[1]

    @pl.loop(0, NCH)
    def _(c):
        for i in range(1, N_MP):
            given(c, i).wait()
        own_given(c).wait()


def hand_over(gf, g6, g7, gf_out, g6_out, g7_out, sem):
    copies = [pltpu.make_async_copy(g6, g6_out, sem.at[N_MP]), pltpu.make_async_copy(g7, g7_out, sem.at[N_MP + 1])]
    for p in range(N_MP):
        rows = pl.ds(p * 4 * UTT, 4 * UTT)
        copies.append(pltpu.make_async_copy(gf.at[rows], gf_out.at[rows], sem.at[p]))
    for copy in copies:
        copy.start()
    for copy in copies:
        copy.wait()


def body(features, conv6_weight, conv7_weight, frame_grads, frame_dest, lengths):
    vmem, hbm = pl.BlockSpec(memory_space=pltpu.VMEM), pl.BlockSpec(memory_space=pl.ANY)
    dma = pltpu.SemaphoreType.DMA
    results = pl.pallas_call(
        kernel,
        out_shape=(
            jax.ShapeDtypeStruct(features.shape, BF16),
            jax.ShapeDtypeStruct(conv6_weight.shape, F32),
            jax.ShapeDtypeStruct(conv7_weight.shape, F32),
        ),
        in_specs=[hbm] * 6,
        out_specs=(hbm, vmem, vmem),
        scratch_shapes=[
            pltpu.VMEM((FRM, CH), BF16),
            pltpu.VMEM((FRM,), jnp.int32),
            pltpu.SMEM((N_MP,), jnp.int32),
            pltpu.VMEM((N_MP, 4 * UTT, CH), BF16),
            pltpu.VMEM((2, 4, 4, 2, KR, C), BF16),
            pltpu.VMEM((8, FRM), jnp.int32),
            pltpu.VMEM((2, 2 * N_DP, 256), F32),
            pltpu.VMEM((FRM, 4 * CH), BF16),
            pltpu.VMEM((N_DP, BLK, CH), BF16),
            pltpu.VMEM((N_DP, BLK, CH), BF16),
            pltpu.VMEM((2, UTT, 2 * CH), F32),
            pltpu.VMEM((N_MP, UTT, CH), BF16),
            pltpu.VMEM((N_MP, UTT, CH), BF16),
            pltpu.VMEM((N_MP, RC, CH), F32),
            pltpu.VMEM((NCH, 2 * FC, 2 * C), BF16),
            pltpu.VMEM((NCH, FC, 2 * C), BF16),
            pltpu.VMEM((NCH, 2 * FC, C), F32),
            pltpu.VMEM((NCH, FC, C), F32),
            pltpu.VMEM((NCH, FC, C), BF16),
            pltpu.VMEM((NCH, 2 * FC, C), BF16),
            pltpu.VMEM((N_MP, 4 * UTT, CH), BF16),
            pltpu.VMEM((2, 4, 4, 2, KR, C), F32),
            pltpu.VMEM((2, 4, 4, KR, C), BF16),
            pltpu.VMEM((2, 4, 4, KR, C), BF16),
            pltpu.VMEM((2, 4, 4, KR, C), BF16),
            pltpu.VMEM((2, 4, 4, KR, C), BF16),
            pltpu.VMEM((2, 4, KR, C), F32),
            pltpu.VMEM((2, 4, KR, C), BF16),
            pltpu.VMEM((2, 4, KR, C), BF16),
            pltpu.VMEM((2, KR, C), F32),
            pltpu.VMEM((N_MP, 2, KR, CH), F32),
            pltpu.VMEM((N_MP, 2, KR, CH), F32),
            dma((4,)), dma((4,)), dma((4,)), dma((4,)), dma((4,)), dma((4,)), dma((4,)), dma((4,)),
            dma((2, 4)), dma((2, 4)), dma((2, 4)), dma((2, 4)), dma((2,)), dma((2,)),
            dma((6,)), dma((NCH, N_MP)), dma((NCH, N_MP)), dma((N_DP,)), dma((N_DP,)), dma((N_MP,)), dma((N_MP,)),
            dma((NCH, N_MP)), dma((NCH, N_MP)), dma((2,)), dma((2,)), dma((2, 4)), dma((2, 4)), dma((2, 4)), dma((2, 4)),
            dma((N_MP,)), dma((N_MP,)),
        ],
        compiler_params=pltpu.CompilerParams(
            collective_id=0, has_side_effects=True, vmem_limit_bytes=56 * 2**20,
            fuse_transposed_lhs_in_matmul=True,
        ),
        name="encoder_backward",
    )(features, conv6_weight, conv7_weight, frame_grads, frame_dest, lengths)
    return pl.pallas_call(
        hand_over,
        out_shape=tuple(jax.ShapeDtypeStruct(r.shape, r.dtype) for r in results),
        in_specs=[hbm] * 3,
        out_specs=(hbm,) * 3,
        scratch_shapes=[dma((N_MP + 2,))],
        name="hand_over",
    )(*results)


def solution(mesh):
    placed = (P("dp", "mp"), P("dp", "mp"), P("dp", "mp"), P("dp", "mp"), P(), P("dp"))
    return jax.shard_map(
        body,
        mesh=mesh,
        in_specs=placed,
        out_specs=(P("dp", "mp"), P("dp", "mp"), P("dp", "mp")),
        check_vma=False,
    )
```

```python
import jax
import jax.numpy as jnp
from jax import lax
from jax.experimental import pallas as pl
from jax.experimental.pallas import tpu as pltpu
from jax.sharding import PartitionSpec as P

C = 512
FRM = 2048
CAP = 192
N_DP = 32
N_MP = 4
CH = C // N_MP
UTT = FRM // N_MP
FC = 128
NCH = UTT // FC
RC = 4 * FC
PARTS = 8
META = 16
BLK = CAP + META
KR = 32

inv_root_two = 0.7071067811865476
inv_root_tau = 0.3989422804014327
F32 = jnp.float32
BF16 = jnp.bfloat16


def dot(left, right, contract=((1,), (0,))):
    return lax.dot_general(left, right, (contract, ((), ())), preferred_element_type=F32)


def iota(shape, axis):
    return lax.broadcasted_iota(jnp.int32, shape, axis)


def kernel(
    feat, w6, w7, grads_in, dest_in, lens_in,
    gf, g6, g7,
    grads, dest, lens, xin, wts, quad, meta, rhs, obox, arrived, placed, exb, mg,
    s32, pairs6, pairs7, slope6, slope7, delta7, delta6, gout,
    gsum, core_out, core_in, part_out, part_in, part, chip_out, chip_in, share, x_out, x_in,
    va_s, va_r, vb_s, vb_r, vx_s, vx_r, ux_s, ux_r, ua_s, ua_r, ub_s, ub_r, wc_s, wc_r, own_sem, f_s, f_r, rt_s, rt_r, ex_s, ex_r,
    go_s, go_r, rc_s, rc_r, ra_s, ra_r, rb_s, rb_r, rx_s, rx_r,
):
    d, m = lax.axis_index("dp"), lax.axis_index("mp")
    z, y, core = lax.div(d, 8), lax.rem(lax.div(d, 2), 4), lax.rem(d, 2)

    def dp_of(dz, dy, dc):
        return lax.rem(z + dz, 4) * 8 + lax.rem(y + dy, 4) * 2 + lax.rem(core + dc, 2)

    def remote(src, dst, send, recv, dp, mp):
        return pltpu.make_async_remote_copy(
            src_ref=src, dst_ref=dst, send_sem=send, recv_sem=recv,
            device_id=(dp, mp), device_id_type=pl.DeviceIdType.MESH,
        )

    barrier = pltpu.get_barrier_semaphore()
    for i in range(1, N_MP):
        pl.semaphore_signal(barrier, inc=1, device_id=(d, lax.rem(m + i, N_MP)), device_id_type=pl.DeviceIdType.MESH)

    @pl.loop(1, N_DP)
    def _(k):
        pl.semaphore_signal(barrier, inc=1, device_id=(lax.rem(d + k, N_DP), m), device_id_type=pl.DeviceIdType.MESH)

    own_rows = pltpu.make_async_copy(
        feat.at[pl.ds(pl.multiple_of(m * 4 * UTT, 4 * UTT), 4 * UTT), :], xin.at[m], own_sem.at[0]
    )
    own_rows.start()
    cols = pl.ds(pl.multiple_of(m * CH, CH), CH)
    local = [
        pltpu.make_async_copy(dest_in.at[pl.ds(pl.multiple_of(d * FRM, FRM), FRM)], dest, own_sem.at[1]),
        pltpu.make_async_copy(grads_in, grads, own_sem.at[2]),
        pltpu.make_async_copy(w6, wts.at[0, z, y, core, :, cols], own_sem.at[3]),
        pltpu.make_async_copy(w7, wts.at[1, z, y, core, :, cols], own_sem.at[4]),
        pltpu.make_async_copy(lens_in, lens, own_sem.at[5]),
    ]
    for copy in local:
        copy.start()
    for copy in local:
        copy.wait()
    pl.semaphore_wait(barrier, N_DP - 1 + N_MP - 1)

    def along_z(i):
        return dp_of(i, 0, 0)

    def along_y(i):
        return dp_of(0, i, 0)

    def va(i):
        block = wts.at[1, z, y, core, :, cols]
        return remote(block, block, va_s.at[i], va_r.at[i], along_y(i), m)

    def vb(i):
        block = wts.at[1, z, :, core, :, cols]
        return remote(block, block, vb_s.at[i], vb_r.at[i], along_z(i), m)

    def vx(i):
        block = wts.at[1, :, :, core, :, cols]
        return remote(block, block, vx_s.at[i], vx_r.at[i], d, lax.rem(m + i, N_MP))

    def ux(i):
        block = wts.at[0, z, y, core, :, cols]
        return remote(block, block, ux_s.at[i], ux_r.at[i], d, lax.rem(m + i, N_MP))

    def ua(h, i):
        block = wts.at[0, z, y, core, :, pl.ds(h * 256, 256)]
        return remote(block, block, ua_s.at[h, i], ua_r.at[h, i], (along_z, along_y)[h](i), m)

    def ub(h, i):
        half = pl.ds(h * 256, 256)
        block = wts.at[0, :, y, core, :, half] if h == 0 else wts.at[0, z, :, core, :, half]
        return remote(block, block, ub_s.at[h, i], ub_r.at[h, i], (along_y, along_z)[h](i), m)

    def wc(w):
        block = wts.at[w, :, :, core]
        return remote(block, block, wc_s.at[w], wc_r.at[w], dp_of(0, 0, 1), m)

    for i in range(1, 4):
        ux(i).start()
        va(i).start()

    def feature(c, i):
        p = lax.rem(m + i, N_MP)
        return remote(
            feat.at[pl.ds(pl.multiple_of(p * 4 * UTT + c * RC, RC), RC), :],
            xin.at[m, pl.ds(pl.multiple_of(c * RC, RC), RC), :],
            f_s.at[c, i], f_r.at[c, i], d, p,
        )

    for c in range(NCH // 2):
        for i in range(1, N_MP):
            feature(c, i).start()

    def number_slots():
        target = dest[...].reshape(1, FRM)
        row = lax.bitwise_and(target, FRM - 1)
        shifted = lambda by, top: lax.bitwise_and(lax.shift_right_logical(target, by), top)
        owner = (
            lax.bitwise_and(shifted(14, 3) - z, 3) * 8
            + lax.bitwise_and(shifted(12, 3) - y, 3) * 2
            + lax.bitwise_and(shifted(11, 1) + core, 1)
        )
        before = jnp.where(iota((256, 256), 0) < iota((256, 256), 1), 1.0, 0.0).astype(BF16)
        carry = jnp.zeros((N_DP, 1), F32)
        ranks = []
        for b in range(FRM // 256):
            mine = owner[:, b * 256 : (b + 1) * 256] == iota((N_DP, 256), 0)
            ones = jnp.where(mine, 1.0, 0.0)
            earlier = dot(ones.astype(BF16), before) + carry
            ranks.append(jnp.sum(jnp.where(mine, earlier, 0.0), axis=0, keepdims=True))
            carry = carry + jnp.sum(ones, axis=1, keepdims=True)
        rank = jnp.concatenate(ranks, axis=1).astype(jnp.int32)
        quad[...] = jnp.where(lax.shift_right_logical(owner, 2) == iota((8, FRM), 0), rank, 4096)
        remainder = jnp.where(lax.bitwise_and(owner, 3) == iota((8, FRM), 0), 1.0, 0.0).astype(BF16)
        spread = jnp.where(iota((8, 4 * CH), 0) == lax.div(iota((8, 4 * CH), 1), CH), 1.0, 0.0).astype(BF16)
        for b in range(FRM // 256):
            part_ = slice(b * 256, (b + 1) * 256)
            keep = dot(remainder[:, part_], spread, ((0,), (0,))).astype(BF16)
            rows = grads[part_, :]
            rhs[part_, :] = keep * jnp.concatenate([rows] * 4, axis=1)
        line = iota((2 * N_DP, FRM), 0)
        digits = jnp.where(
            line == owner, lax.shift_right_logical(row, 8),
            jnp.where(line == owner + N_DP, lax.bitwise_and(row, 255), 0),
        ).astype(F32).astype(BF16)
        for odd in range(2):
            pick = jnp.where(iota((256, FRM), 0) == rank + 64 * odd, 1.0, 0.0).astype(BF16)
            meta[odd] = dot(digits, pick, ((1,), (1,)))

    number_slots()
    for i in range(1, 4):
        va(i).wait()
        ux(i).wait()
    for i in range(1, 4):
        vb(i).start()
        ua(0, i).start()
        ua(1, i).start()

    def routed(k):
        return remote(
            obox.at[k], arrived.at[k], rt_s.at[k], rt_r.at[k],
            dp_of(lax.div(k, 8), lax.rem(lax.div(k, 2), 4), lax.rem(k, 2)), m,
        )

    own_block = pltpu.make_async_copy(obox.at[0], arrived.at[0], rt_r.at[0])

    def pack(g):
        pick = jnp.where(iota((CAP, FRM), 0) == quad[pl.ds(g, 1), :], 1.0, 0.0).astype(BF16)
        both = dot(pick, rhs[...])
        line = iota((META, 128), 0)
        for j in range(4):
            k = g * 4 + j
            obox[k, 0:CAP, :] = both[:, j * CH : (j + 1) * CH].astype(BF16)
            high, low = meta[j % 2, pl.ds(k, 1), :], meta[j % 2, pl.ds(k + N_DP, 1), :]
            tile = jnp.where(line == 0, high[:, :128], jnp.where(line == 1, high[:, 128:], 0.0))
            tile = jnp.where(line == 2, low[:, :128], jnp.where(line == 3, low[:, 128:], tile))
            obox[k, CAP:BLK, :] = tile.astype(BF16)

    @pl.loop(0, 8)
    def _(i):
        g = lax.rem(5 * i + 2, 8)
        pack(g)
        for j in range(1, 4):
            routed(g * 4 + j).start()

        @pl.when(g != 0)
        def _():
            routed(g * 4).start()

        @pl.when(g == 0)
        def _():
            own_block.start()

    for i in range(1, 4):
        vb(i).wait()
        ua(0, i).wait()
        ua(1, i).wait()
    for i in range(1, 4):
        vx(i).start()
        ub(0, i).start()
        ub(1, i).start()
    for c in range(NCH // 2, NCH):
        for i in range(1, N_MP):
            feature(c, i).start()

    def place(g):
        first, second = [], []
        for i in range(4):
            digits = arrived[g * 4 + i, CAP:BLK, :].astype(F32)
            first.append(digits[0:1] * 256.0 + digits[2:3])
            second.append(digits[1:2] * 256.0 + digits[3:4])
        left = iota((1, 128), 1) < 64
        at = jnp.concatenate(
            [
                first[0], jnp.where(left, second[0], first[1]), second[1],
                first[2], jnp.where(left, second[2], first[3]), second[3],
            ],
            axis=1,
        ).astype(jnp.int32)
        half = lax.shift_right_logical(at, 10)
        within = lax.bitwise_and(at, 1023)
        top = jnp.where(iota((8, 4 * CAP), 0) == 0, half, 0).astype(F32).astype(BF16)
        later = dot(top, jnp.ones((8, CH), BF16), ((0,), (0,))).astype(BF16)
        block = arrived[pl.ds(g * 4, 4), 0:CAP, :].reshape(4 * CAP, CH)
        second_half = block * later
        sides = jnp.concatenate([block - second_half, second_half], axis=1)
        for a in range(2):
            pick = jnp.where(iota((UTT, 4 * CAP), 0) + a * UTT == within, 1.0, 0.0).astype(BF16)
            placed[a] += dot(pick, sides)

    placed[...] = jnp.zeros((2, UTT, 2 * CH), F32)

    @pl.loop(0, 8)
    def _(i):
        g = lax.rem(5 * i + 2, 8)
        for j in range(1, 4):
            routed(g * 4 + j).wait()

        @pl.when(g != 0)
        def _():
            routed(g * 4).wait()

        @pl.when(g == 0)
        def _():
            own_block.wait()

        place(g)

    def exchange(i):
        p = lax.rem(m + i, N_MP)
        return remote(exb.at[p], mg.at[m], ex_s.at[i], ex_r.at[i], d, p)

    for p in range(N_MP):
        exb[p] = placed[p % 2, :, (p // 2) * CH : (p // 2 + 1) * CH].astype(BF16)
    for i in range(1, N_MP):
        exchange(i).start()
    mg[m] = exb[m]

    for i in range(1, 4):
        ub(0, i).wait()
        ub(1, i).wait()
    wc(0).start()
    for i in range(1, 4):
        vx(i).wait()
    wc(1).start()
    own_rows.wait()

    def unpair(c):
        rows = pl.ds(pl.multiple_of(c * RC, RC), RC)
        for g in range(N_MP):
            s32[g] = xin[g, rows, :].astype(F32)
        for j in range(4):
            for g in range(N_MP):
                lanes = slice((j % 2) * C + g * CH, (j % 2) * C + (g + 1) * CH)
                pairs6[c, (j // 2) * FC : (j // 2 + 1) * FC, lanes] = s32[g, pl.ds(j, FC, stride=4), :].astype(BF16)

    def forward(c):
        pre = dot(pairs6[c], wts[0].reshape(2 * C, C))
        half = 0.5 * (1.0 + lax.erf(pre * inv_root_two))
        act = (pre * half).astype(BF16)
        slope6[c] = half + pre * jnp.exp(-0.5 * pre * pre) * inv_root_tau
        pairs7[c, :, 0:C] = act[:FC]
        pairs7[c, :, C : 2 * C] = act[FC:]
        pre = dot(pairs7[c], wts[1].reshape(2 * C, C))
        half = 0.5 * (1.0 + lax.erf(pre * inv_root_two))
        slope7[c] = half + pre * jnp.exp(-0.5 * pre * pre) * inv_root_tau

    for c in range(2):
        for i in range(1, N_MP):
            feature(c, i).wait()
        unpair(c)
    for w in range(2):
        wc(w).wait()
    for c in range(NCH):
        if c >= 2:
            for i in range(1, N_MP):
                feature(c, i).wait()
            unpair(c)
        forward(c)

    for i in range(1, N_MP):
        exchange(i).wait()

    valid = lax.div(lens[m] - 400, 320) + 1

    def given(c, i):
        p = lax.rem(m + i, N_MP)
        return remote(
            gout.at[p, pl.ds(pl.multiple_of(c * RC, RC), RC), :],
            gf.at[pl.ds(pl.multiple_of(m * 4 * UTT + c * RC, RC), RC), :],
            go_s.at[c, i], go_r.at[c, i], d, p,
        )

    def own_given(c):
        return pltpu.make_async_copy(
            gout.at[m, pl.ds(pl.multiple_of(c * RC, RC), RC), :],
            gf.at[pl.ds(pl.multiple_of(m * 4 * UTT + c * RC, RC), RC), :],
            go_s.at[c, 0],
        )

    def backward(c):
        frames = pl.ds(pl.multiple_of(c * FC, FC), FC)
        live = iota((FC, CH), 0) + c * FC < valid
        for g in range(N_MP):
            lanes = slice(g * CH, (g + 1) * CH)
            coming = jnp.where(live, mg[g, frames, :].astype(F32), 0.0)
            delta7[c, :, lanes] = (coming * slope7[c, :, lanes]).astype(BF16)
        back = dot(delta7[c], wts[1].reshape(2 * C, C), ((1,), (1,)))
        delta6[c, 0:FC, :] = (back[:, :C] * slope6[c, 0:FC, :]).astype(BF16)
        delta6[c, FC : 2 * FC, :] = (back[:, C:] * slope6[c, FC : 2 * FC, :]).astype(BF16)
        back = dot(delta6[c], wts[0].reshape(2 * C, C), ((1,), (1,)))
        for j in range(4):
            for g in range(N_MP):
                s32[g, pl.ds(j, FC, stride=4), :] = back[
                    (j // 2) * FC : (j // 2 + 1) * FC, (j % 2) * C + g * CH : (j % 2) * C + (g + 1) * CH
                ]
        for g in range(N_MP):
            gout[g, pl.ds(pl.multiple_of(c * RC, RC), RC), :] = s32[g].astype(BF16)

    @pl.loop(0, NCH)
    def _(c):
        backward(c)
        for i in range(1, N_MP):
            given(c, i).start()
        own_given(c).start()

    def terms(w, b):
        pairs, deltas, count = ((pairs6, delta6, 2 * UTT), (pairs7, delta7, UTT))[w]
        left = pairs[:, :, pl.ds(pl.multiple_of(b * 256, 256), 256)].reshape(count, 256)
        right = deltas[...].reshape(count, C)
        gsum[w, b] = dot(left, right, ((0,), (0,))).reshape(4, 2, KR, C)

    def to_mate(w):
        return remote(core_out.at[w], core_in.at[w], rc_s.at[w], rc_r.at[w], dp_of(0, 0, 1), m)

    def ra(w, i):
        p = lax.rem((z, y)[w] + i, 4)
        return remote(
            part_out.at[w, p], part_in.at[w, i], ra_s.at[w, i], ra_r.at[w, i], (along_z, along_y)[w](i), m
        )

    def rb(w, i):
        p = lax.rem((y, z)[w] + i, 4)
        return remote(
            chip_out.at[w, p], chip_in.at[w, i], rb_s.at[w, i], rb_r.at[w, i], (along_y, along_z)[w](i), m
        )

    for w in (1, 0):

        @pl.loop(0, 4)
        def _(b):
            terms(w, b)
            core_out[w, b] = gsum[w, b, :, 1 - core].astype(BF16)

        to_mate(w).start()

    for w in (1, 0):
        to_mate(w).wait()

        @pl.loop(0, 4)
        def _(a):
            for b in range(4):
                zy = (a, b) if w == 0 else (b, a)
                total = gsum[w, zy[0], zy[1], core] + core_in[w, zy[0], zy[1]].astype(F32)
                part_out[w, a, b] = total.astype(BF16)

        for i in range(1, 4):
            ra(w, i).start()

    for w in (1, 0):
        for b in range(4):
            zy = (z, b) if w == 0 else (b, y)
            part[w, b] = gsum[w, zy[0], zy[1], core] + core_in[w, zy[0], zy[1]].astype(F32)
        for i in range(1, 4):
            ra(w, i).wait()
            part[w] += part_in[w, i].astype(F32)
        chip_out[w] = part[w].astype(BF16)
        for i in range(1, 4):
            rb(w, i).start()

    for w in (1, 0):
        share[w] = part[w, (y, z)[w]]
        for i in range(1, 4):
            rb(w, i).wait()
            share[w] += chip_in[w, i].astype(F32)
    for g in range(N_MP):
        x_out[g] = share[:, :, g * CH : (g + 1) * CH]

    def along(i):
        p = lax.rem(m + i, N_MP)
        return remote(x_out.at[p], x_in.at[i], rx_s.at[i], rx_r.at[i], d, p)

    for i in range(1, N_MP):
        along(i).start()
    total = x_out[m]
    for i in range(1, N_MP):
        along(i).wait()
        total = total + x_in[i]
    g6[...] = total[0]
    g7[...] = total[1]

    @pl.loop(0, NCH)
    def _(c):
        for i in range(1, N_MP):
            given(c, i).wait()
        own_given(c).wait()


def hand_over(gf, g6, g7, gf_out, g6_out, g7_out, held, held6, held7, sem_in, sem_out):
    steps = [(g6, held6, g6_out), (g7, held7, g7_out)]
    for p in range(PARTS):
        rows = pl.ds(p * (16 * UTT // PARTS), 16 * UTT // PARTS)
        steps.append((gf.at[rows], held.at[rows], gf_out.at[rows]))
    come = [pltpu.make_async_copy(a, b, sem_in.at[n]) for n, (a, b, _) in enumerate(steps)]
    go = [pltpu.make_async_copy(b, c, sem_out.at[n]) for n, (_, b, c) in enumerate(steps)]
    for copy in come:
        copy.start()
    for here, there in zip(come, go):
        here.wait()
        there.start()
    for copy in go:
        copy.wait()


def body(features, conv6_weight, conv7_weight, frame_grads, frame_dest, lengths):
    vmem, hbm = pl.BlockSpec(memory_space=pltpu.VMEM), pl.BlockSpec(memory_space=pl.ANY)
    dma = pltpu.SemaphoreType.DMA
    results = pl.pallas_call(
        kernel,
        out_shape=(
            jax.ShapeDtypeStruct(features.shape, BF16),
            jax.ShapeDtypeStruct(conv6_weight.shape, F32),
            jax.ShapeDtypeStruct(conv7_weight.shape, F32),
        ),
        in_specs=[hbm] * 6,
        out_specs=(hbm, vmem, vmem),
        scratch_shapes=[
            pltpu.VMEM((FRM, CH), BF16),
            pltpu.VMEM((FRM,), jnp.int32),
            pltpu.SMEM((N_MP,), jnp.int32),
            pltpu.VMEM((N_MP, 4 * UTT, CH), BF16),
            pltpu.VMEM((2, 4, 4, 2, KR, C), BF16),
            pltpu.VMEM((8, FRM), jnp.int32),
            pltpu.VMEM((2, 2 * N_DP, 256), F32),
            pltpu.VMEM((FRM, 4 * CH), BF16),
            pltpu.VMEM((N_DP, BLK, CH), BF16),
            pltpu.VMEM((N_DP, BLK, CH), BF16),
            pltpu.VMEM((2, UTT, 2 * CH), F32),
            pltpu.VMEM((N_MP, UTT, CH), BF16),
            pltpu.VMEM((N_MP, UTT, CH), BF16),
            pltpu.VMEM((N_MP, RC, CH), F32),
            pltpu.VMEM((NCH, 2 * FC, 2 * C), BF16),
            pltpu.VMEM((NCH, FC, 2 * C), BF16),
            pltpu.VMEM((NCH, 2 * FC, C), F32),
            pltpu.VMEM((NCH, FC, C), F32),
            pltpu.VMEM((NCH, FC, C), BF16),
            pltpu.VMEM((NCH, 2 * FC, C), BF16),
            pltpu.VMEM((N_MP, 4 * UTT, CH), BF16),
            pltpu.VMEM((2, 4, 4, 2, KR, C), F32),
            pltpu.VMEM((2, 4, 4, KR, C), BF16),
            pltpu.VMEM((2, 4, 4, KR, C), BF16),
            pltpu.VMEM((2, 4, 4, KR, C), BF16),
            pltpu.VMEM((2, 4, 4, KR, C), BF16),
            pltpu.VMEM((2, 4, KR, C), F32),
            pltpu.VMEM((2, 4, KR, C), BF16),
            pltpu.VMEM((2, 4, KR, C), BF16),
            pltpu.VMEM((2, KR, C), F32),
            pltpu.VMEM((N_MP, 2, KR, CH), F32),
            pltpu.VMEM((N_MP, 2, KR, CH), F32),
            dma((4,)), dma((4,)), dma((4,)), dma((4,)), dma((4,)), dma((4,)), dma((4,)), dma((4,)),
            dma((2, 4)), dma((2, 4)), dma((2, 4)), dma((2, 4)), dma((2,)), dma((2,)),
            dma((6,)), dma((NCH, N_MP)), dma((NCH, N_MP)), dma((N_DP,)), dma((N_DP,)), dma((N_MP,)), dma((N_MP,)),
            dma((NCH, N_MP)), dma((NCH, N_MP)), dma((2,)), dma((2,)), dma((2, 4)), dma((2, 4)), dma((2, 4)), dma((2, 4)),
            dma((N_MP,)), dma((N_MP,)),
        ],
        compiler_params=pltpu.CompilerParams(
            collective_id=0, has_side_effects=True, vmem_limit_bytes=56 * 2**20,
            fuse_transposed_lhs_in_matmul=True,
        ),
        name="encoder_backward",
    )(features, conv6_weight, conv7_weight, frame_grads, frame_dest, lengths)
    return pl.pallas_call(
        hand_over,
        out_shape=tuple(jax.ShapeDtypeStruct(r.shape, r.dtype) for r in results),
        in_specs=[hbm] * 3,
        out_specs=(hbm,) * 3,
        scratch_shapes=[
            pltpu.VMEM((16 * UTT, CH), BF16), pltpu.VMEM((KR, CH), F32), pltpu.VMEM((KR, CH), F32),
            dma((PARTS + 2,)), dma((PARTS + 2,)),
        ],
        name="hand_over",
    )(*results)


def solution(mesh):
    placed = (P("dp", "mp"), P("dp", "mp"), P("dp", "mp"), P("dp", "mp"), P(), P("dp"))
    return jax.shard_map(
        body,
        mesh=mesh,
        in_specs=placed,
        out_specs=(P("dp", "mp"), P("dp", "mp"), P("dp", "mp")),
        check_vma=False,
    )
```

```python
import jax
import jax.numpy as jnp
from jax import lax
from jax.experimental import pallas as pl
from jax.experimental.pallas import tpu as pltpu
from jax.sharding import PartitionSpec as P

C = 512
FRM = 2048
CAP = 192
N_DP = 32
N_MP = 4
CH = C // N_MP
UTT = FRM // N_MP
FC = 128
NCH = UTT // FC
RC = 4 * FC
PARTS = 8
META = 16
BLK = CAP + META
KR = 32

inv_root_two = 0.7071067811865476
inv_root_tau = 0.3989422804014327
F32 = jnp.float32
BF16 = jnp.bfloat16


def dot(left, right, contract=((1,), (0,))):
    return lax.dot_general(left, right, (contract, ((), ())), preferred_element_type=F32)


def iota(shape, axis):
    return lax.broadcasted_iota(jnp.int32, shape, axis)


def kernel(
    feat, w6, w7, grads_in, dest_in, lens_in,
    gf, g6, g7,
    grads, dest, lens, xin, wts, quad, meta, rhs, obox, arrived, placed, exb, mg,
    s32, pairs6, pairs7, slope6, slope7, delta7, delta6, gout,
    gsum, core_out, core_in, part_out, part_in, part, chip_out, chip_in, share, x_out, x_in,
    va_s, va_r, vb_s, vb_r, vx_s, vx_r, ux_s, ux_r, ua_s, ua_r, ub_s, ub_r, wc_s, wc_r, own_sem, f_s, f_r, rt_s, rt_r, ex_s, ex_r,
    go_s, go_r, rc_s, rc_r, ra_s, ra_r, rb_s, rb_r, rx_s, rx_r,
):
    d, m = lax.axis_index("dp"), lax.axis_index("mp")
    z, y, core = lax.div(d, 8), lax.rem(lax.div(d, 2), 4), lax.rem(d, 2)

    def dp_of(dz, dy, dc):
        return lax.rem(z + dz, 4) * 8 + lax.rem(y + dy, 4) * 2 + lax.rem(core + dc, 2)

    def remote(src, dst, send, recv, dp, mp):
        return pltpu.make_async_remote_copy(
            src_ref=src, dst_ref=dst, send_sem=send, recv_sem=recv,
            device_id=(dp, mp), device_id_type=pl.DeviceIdType.MESH,
        )

    barrier = pltpu.get_barrier_semaphore()
    for i in range(1, N_MP):
        pl.semaphore_signal(barrier, inc=1, device_id=(d, lax.rem(m + i, N_MP)), device_id_type=pl.DeviceIdType.MESH)

    @pl.loop(1, N_DP)
    def _(k):
        pl.semaphore_signal(barrier, inc=1, device_id=(lax.rem(d + k, N_DP), m), device_id_type=pl.DeviceIdType.MESH)

    own_rows = pltpu.make_async_copy(
        feat.at[pl.ds(pl.multiple_of(m * 4 * UTT, 4 * UTT), 4 * UTT), :], xin.at[m], own_sem.at[0]
    )
    own_rows.start()
    cols = pl.ds(pl.multiple_of(m * CH, CH), CH)
    local = [
        pltpu.make_async_copy(dest_in.at[pl.ds(pl.multiple_of(d * FRM, FRM), FRM)], dest, own_sem.at[1]),
        pltpu.make_async_copy(grads_in, grads, own_sem.at[2]),
        pltpu.make_async_copy(w6, wts.at[0, z, y, core, :, cols], own_sem.at[3]),
        pltpu.make_async_copy(w7, wts.at[1, z, y, core, :, cols], own_sem.at[4]),
        pltpu.make_async_copy(lens_in, lens, own_sem.at[5]),
    ]
    for copy in local:
        copy.start()
    for copy in local:
        copy.wait()
    pl.semaphore_wait(barrier, N_DP - 1 + N_MP - 1)

    def along_z(i):
        return dp_of(i, 0, 0)

    def along_y(i):
        return dp_of(0, i, 0)

    def va(i):
        block = wts.at[1, z, y, core, :, cols]
        return remote(block, block, va_s.at[i], va_r.at[i], along_y(i), m)

    def vb(i):
        block = wts.at[1, z, :, core, :, cols]
        return remote(block, block, vb_s.at[i], vb_r.at[i], along_z(i), m)

    def vx(i):
        block = wts.at[1, :, :, core, :, cols]
        return remote(block, block, vx_s.at[i], vx_r.at[i], d, lax.rem(m + i, N_MP))

    def ux(i):
        block = wts.at[0, z, y, core, :, cols]
        return remote(block, block, ux_s.at[i], ux_r.at[i], d, lax.rem(m + i, N_MP))

    def ua(h, i):
        block = wts.at[0, z, y, core, :, pl.ds(h * 256, 256)]
        return remote(block, block, ua_s.at[h, i], ua_r.at[h, i], (along_z, along_y)[h](i), m)

    def ub(h, i):
        half = pl.ds(h * 256, 256)
        block = wts.at[0, :, y, core, :, half] if h == 0 else wts.at[0, z, :, core, :, half]
        return remote(block, block, ub_s.at[h, i], ub_r.at[h, i], (along_y, along_z)[h](i), m)

    def wc(w):
        block = wts.at[w, :, :, core]
        return remote(block, block, wc_s.at[w], wc_r.at[w], dp_of(0, 0, 1), m)

    for i in range(1, 4):
        ux(i).start()
        va(i).start()

    def feature(c, i):
        p = lax.rem(m + i, N_MP)
        return remote(
            feat.at[pl.ds(pl.multiple_of(p * 4 * UTT + c * RC, RC), RC), :],
            xin.at[m, pl.ds(pl.multiple_of(c * RC, RC), RC), :],
            f_s.at[c, i], f_r.at[c, i], d, p,
        )

    for c in range(NCH // 2):
        for i in range(1, N_MP):
            feature(c, i).start()

    def number_slots():
        target = dest[...].reshape(1, FRM)
        row = lax.bitwise_and(target, FRM - 1)
        shifted = lambda by, top: lax.bitwise_and(lax.shift_right_logical(target, by), top)
        owner = (
            lax.bitwise_and(shifted(14, 3) - z, 3) * 8
            + lax.bitwise_and(shifted(12, 3) - y, 3) * 2
            + lax.bitwise_and(shifted(11, 1) + core, 1)
        )
        before = jnp.where(iota((256, 256), 0) < iota((256, 256), 1), 1.0, 0.0).astype(BF16)
        carry = jnp.zeros((N_DP, 1), F32)
        ranks = []
        for b in range(FRM // 256):
            mine = owner[:, b * 256 : (b + 1) * 256] == iota((N_DP, 256), 0)
            ones = jnp.where(mine, 1.0, 0.0)
            earlier = dot(ones.astype(BF16), before) + carry
            ranks.append(jnp.sum(jnp.where(mine, earlier, 0.0), axis=0, keepdims=True))
            carry = carry + jnp.sum(ones, axis=1, keepdims=True)
        rank = jnp.concatenate(ranks, axis=1).astype(jnp.int32)
        quad[...] = jnp.where(lax.shift_right_logical(owner, 2) == iota((8, FRM), 0), rank, 4096)
        remainder = jnp.where(lax.bitwise_and(owner, 3) == iota((8, FRM), 0), 1.0, 0.0).astype(BF16)
        spread = jnp.where(iota((8, 4 * CH), 0) == lax.div(iota((8, 4 * CH), 1), CH), 1.0, 0.0).astype(BF16)
        for b in range(FRM // 256):
            part_ = slice(b * 256, (b + 1) * 256)
            keep = dot(remainder[:, part_], spread, ((0,), (0,))).astype(BF16)
            rows = grads[part_, :]
            rhs[part_, :] = keep * jnp.concatenate([rows] * 4, axis=1)
        line = iota((2 * N_DP, FRM), 0)
        digits = jnp.where(
            line == owner, lax.shift_right_logical(row, 8),
            jnp.where(line == owner + N_DP, lax.bitwise_and(row, 255), 0),
        ).astype(F32).astype(BF16)
        for odd in range(2):
            pick = jnp.where(iota((256, FRM), 0) == rank + 64 * odd, 1.0, 0.0).astype(BF16)
            meta[odd] = dot(digits, pick, ((1,), (1,)))

    number_slots()
    for i in range(1, 4):
        va(i).wait()
        ux(i).wait()
    for i in range(1, 4):
        vb(i).start()
        ua(0, i).start()
        ua(1, i).start()

    def routed(k):
        return remote(
            obox.at[k], arrived.at[k], rt_s.at[k], rt_r.at[k],
            dp_of(lax.div(k, 8), lax.rem(lax.div(k, 2), 4), lax.rem(k, 2)), m,
        )

    own_block = pltpu.make_async_copy(obox.at[0], arrived.at[0], rt_r.at[0])

    def pack(g):
        pick = jnp.where(iota((CAP, FRM), 0) == quad[pl.ds(g, 1), :], 1.0, 0.0).astype(BF16)
        both = dot(pick, rhs[...])
        line = iota((META, 128), 0)
        for j in range(4):
            k = g * 4 + j
            obox[k, 0:CAP, :] = both[:, j * CH : (j + 1) * CH].astype(BF16)
            high, low = meta[j % 2, pl.ds(k, 1), :], meta[j % 2, pl.ds(k + N_DP, 1), :]
            tile = jnp.where(line == 0, high[:, :128], jnp.where(line == 1, high[:, 128:], 0.0))
            tile = jnp.where(line == 2, low[:, :128], jnp.where(line == 3, low[:, 128:], tile))
            obox[k, CAP:BLK, :] = tile.astype(BF16)

    @pl.loop(0, 8)
    def _(i):
        g = lax.rem(5 * i + 2, 8)
        pack(g)
        for j in range(1, 4):
            routed(g * 4 + j).start()

        @pl.when(g != 0)
        def _():
            routed(g * 4).start()

        @pl.when(g == 0)
        def _():
            own_block.start()

    for i in range(1, 4):
        vb(i).wait()
        ua(0, i).wait()
        ua(1, i).wait()
    for i in range(1, 4):
        vx(i).start()
    for c in range(NCH // 2, NCH):
        for i in range(1, N_MP):
            feature(c, i).start()

    def place(g):
        first, second = [], []
        for i in range(4):
            digits = arrived[g * 4 + i, CAP:BLK, :].astype(F32)
            first.append(digits[0:1] * 256.0 + digits[2:3])
            second.append(digits[1:2] * 256.0 + digits[3:4])
        left = iota((1, 128), 1) < 64
        at = jnp.concatenate(
            [
                first[0], jnp.where(left, second[0], first[1]), second[1],
                first[2], jnp.where(left, second[2], first[3]), second[3],
            ],
            axis=1,
        ).astype(jnp.int32)
        half = lax.shift_right_logical(at, 10)
        within = lax.bitwise_and(at, 1023)
        top = jnp.where(iota((8, 4 * CAP), 0) == 0, half, 0).astype(F32).astype(BF16)
        later = dot(top, jnp.ones((8, CH), BF16), ((0,), (0,))).astype(BF16)
        block = arrived[pl.ds(g * 4, 4), 0:CAP, :].reshape(4 * CAP, CH)
        second_half = block * later
        sides = jnp.concatenate([block - second_half, second_half], axis=1)
        for a in range(2):
            pick = jnp.where(iota((UTT, 4 * CAP), 0) + a * UTT == within, 1.0, 0.0).astype(BF16)
            placed[a] += dot(pick, sides)

    placed[...] = jnp.zeros((2, UTT, 2 * CH), F32)

    @pl.loop(0, 8)
    def _(i):
        g = lax.rem(5 * i + 2, 8)
        for j in range(1, 4):
            routed(g * 4 + j).wait()

        @pl.when(g != 0)
        def _():
            routed(g * 4).wait()

        @pl.when(g == 0)
        def _():
            own_block.wait()

        place(g)

        @pl.when(i == 3)
        def _():
            for n in range(1, 4):
                ub(0, n).start()
                ub(1, n).start()

    def exchange(i):
        p = lax.rem(m + i, N_MP)
        return remote(exb.at[p], mg.at[m], ex_s.at[i], ex_r.at[i], d, p)

    for p in range(N_MP):
        exb[p] = placed[p % 2, :, (p // 2) * CH : (p // 2 + 1) * CH].astype(BF16)
    for i in range(1, N_MP):
        exchange(i).start()
    mg[m] = exb[m]

    for i in range(1, 4):
        ub(0, i).wait()
        ub(1, i).wait()
    wc(0).start()
    for i in range(1, 4):
        vx(i).wait()
    wc(1).start()
    own_rows.wait()

    def unpair(c):
        rows = pl.ds(pl.multiple_of(c * RC, RC), RC)
        for g in range(N_MP):
            s32[g] = xin[g, rows, :].astype(F32)
        for j in range(4):
            for g in range(N_MP):
                lanes = slice((j % 2) * C + g * CH, (j % 2) * C + (g + 1) * CH)
                pairs6[c, (j // 2) * FC : (j // 2 + 1) * FC, lanes] = s32[g, pl.ds(j, FC, stride=4), :].astype(BF16)

    def forward(c):
        pre = dot(pairs6[c], wts[0].reshape(2 * C, C))
        half = 0.5 * (1.0 + lax.erf(pre * inv_root_two))
        act = (pre * half).astype(BF16)
        slope6[c] = half + pre * jnp.exp(-0.5 * pre * pre) * inv_root_tau
        pairs7[c, :, 0:C] = act[:FC]
        pairs7[c, :, C : 2 * C] = act[FC:]
        pre = dot(pairs7[c], wts[1].reshape(2 * C, C))
        half = 0.5 * (1.0 + lax.erf(pre * inv_root_two))
        slope7[c] = half + pre * jnp.exp(-0.5 * pre * pre) * inv_root_tau

    for c in range(NCH):
        for i in range(1, N_MP):
            feature(c, i).wait()
        unpair(c)
    for w in range(2):
        wc(w).wait()
    for c in range(NCH):
        forward(c)

    for i in range(1, N_MP):
        exchange(i).wait()

    valid = lax.div(lens[m] - 400, 320) + 1

    def given(c, i):
        p = lax.rem(m + i, N_MP)
        return remote(
            gout.at[p, pl.ds(pl.multiple_of(c * RC, RC), RC), :],
            gf.at[pl.ds(pl.multiple_of(m * 4 * UTT + c * RC, RC), RC), :],
            go_s.at[c, i], go_r.at[c, i], d, p,
        )

    def own_given(c):
        return pltpu.make_async_copy(
            gout.at[m, pl.ds(pl.multiple_of(c * RC, RC), RC), :],
            gf.at[pl.ds(pl.multiple_of(m * 4 * UTT + c * RC, RC), RC), :],
            go_s.at[c, 0],
        )

    def backward(c):
        frames = pl.ds(pl.multiple_of(c * FC, FC), FC)
        live = iota((FC, CH), 0) + c * FC < valid
        for g in range(N_MP):
            lanes = slice(g * CH, (g + 1) * CH)
            coming = jnp.where(live, mg[g, frames, :].astype(F32), 0.0)
            delta7[c, :, lanes] = (coming * slope7[c, :, lanes]).astype(BF16)
        back = dot(delta7[c], wts[1].reshape(2 * C, C), ((1,), (1,)))
        delta6[c, 0:FC, :] = (back[:, :C] * slope6[c, 0:FC, :]).astype(BF16)
        delta6[c, FC : 2 * FC, :] = (back[:, C:] * slope6[c, FC : 2 * FC, :]).astype(BF16)
        back = dot(delta6[c], wts[0].reshape(2 * C, C), ((1,), (1,)))
        for j in range(4):
            for g in range(N_MP):
                s32[g, pl.ds(j, FC, stride=4), :] = back[
                    (j // 2) * FC : (j // 2 + 1) * FC, (j % 2) * C + g * CH : (j % 2) * C + (g + 1) * CH
                ]
        for g in range(N_MP):
            gout[g, pl.ds(pl.multiple_of(c * RC, RC), RC), :] = s32[g].astype(BF16)

    @pl.loop(0, NCH)
    def _(c):
        backward(c)
        for i in range(1, N_MP):
            given(c, i).start()
        own_given(c).start()

    def terms(w, b):
        pairs, deltas, count = ((pairs6, delta6, 2 * UTT), (pairs7, delta7, UTT))[w]
        left = pairs[:, :, pl.ds(pl.multiple_of(b * 256, 256), 256)].reshape(count, 256)
        right = deltas[...].reshape(count, C)
        gsum[w, b] = dot(left, right, ((0,), (0,))).reshape(4, 2, KR, C)

    def to_mate(w):
        return remote(core_out.at[w], core_in.at[w], rc_s.at[w], rc_r.at[w], dp_of(0, 0, 1), m)

    def ra(w, i):
        p = lax.rem((z, y)[w] + i, 4)
        return remote(
            part_out.at[w, p], part_in.at[w, i], ra_s.at[w, i], ra_r.at[w, i], (along_z, along_y)[w](i), m
        )

    def rb(w, i):
        p = lax.rem((y, z)[w] + i, 4)
        return remote(
            chip_out.at[w, p], chip_in.at[w, i], rb_s.at[w, i], rb_r.at[w, i], (along_y, along_z)[w](i), m
        )

    for w in (1, 0):

        @pl.loop(0, 4)
        def _(b):
            terms(w, b)
            core_out[w, b] = gsum[w, b, :, 1 - core].astype(BF16)

        to_mate(w).start()

    for w in (1, 0):
        to_mate(w).wait()

        @pl.loop(0, 4)
        def _(a):
            for b in range(4):
                zy = (a, b) if w == 0 else (b, a)
                total = gsum[w, zy[0], zy[1], core] + core_in[w, zy[0], zy[1]].astype(F32)
                part_out[w, a, b] = total.astype(BF16)

        for i in range(1, 4):
            ra(w, i).start()

    for w in (1, 0):
        for b in range(4):
            zy = (z, b) if w == 0 else (b, y)
            part[w, b] = gsum[w, zy[0], zy[1], core] + core_in[w, zy[0], zy[1]].astype(F32)
        for i in range(1, 4):
            ra(w, i).wait()
            part[w] += part_in[w, i].astype(F32)
        chip_out[w] = part[w].astype(BF16)
        for i in range(1, 4):
            rb(w, i).start()

    for w in (1, 0):
        share[w] = part[w, (y, z)[w]]
        for i in range(1, 4):
            rb(w, i).wait()
            share[w] += chip_in[w, i].astype(F32)
    for g in range(N_MP):
        x_out[g] = share[:, :, g * CH : (g + 1) * CH]

    def along(i):
        p = lax.rem(m + i, N_MP)
        return remote(x_out.at[p], x_in.at[i], rx_s.at[i], rx_r.at[i], d, p)

    for i in range(1, N_MP):
        along(i).start()
    total = x_out[m]
    for i in range(1, N_MP):
        along(i).wait()
        total = total + x_in[i]
    g6[...] = total[0]
    g7[...] = total[1]

    @pl.loop(0, NCH)
    def _(c):
        for i in range(1, N_MP):
            given(c, i).wait()
        own_given(c).wait()


def hand_over(gf, g6, g7, gf_out, g6_out, g7_out, held, held6, held7, sem_in, sem_out):
    steps = [(g6, held6, g6_out), (g7, held7, g7_out)]
    for p in range(PARTS):
        rows = pl.ds(p * (16 * UTT // PARTS), 16 * UTT // PARTS)
        steps.append((gf.at[rows], held.at[rows], gf_out.at[rows]))
    come = [pltpu.make_async_copy(a, b, sem_in.at[n]) for n, (a, b, _) in enumerate(steps)]
    go = [pltpu.make_async_copy(b, c, sem_out.at[n]) for n, (_, b, c) in enumerate(steps)]
    for copy in come:
        copy.start()
    for here, there in zip(come, go):
        here.wait()
        there.start()
    for copy in go:
        copy.wait()


def body(features, conv6_weight, conv7_weight, frame_grads, frame_dest, lengths):
    vmem, hbm = pl.BlockSpec(memory_space=pltpu.VMEM), pl.BlockSpec(memory_space=pl.ANY)
    dma = pltpu.SemaphoreType.DMA
    results = pl.pallas_call(
        kernel,
        out_shape=(
            jax.ShapeDtypeStruct(features.shape, BF16),
            jax.ShapeDtypeStruct(conv6_weight.shape, F32),
            jax.ShapeDtypeStruct(conv7_weight.shape, F32),
        ),
        in_specs=[hbm] * 6,
        out_specs=(hbm, vmem, vmem),
        scratch_shapes=[
            pltpu.VMEM((FRM, CH), BF16),
            pltpu.VMEM((FRM,), jnp.int32),
            pltpu.SMEM((N_MP,), jnp.int32),
            pltpu.VMEM((N_MP, 4 * UTT, CH), BF16),
            pltpu.VMEM((2, 4, 4, 2, KR, C), BF16),
            pltpu.VMEM((8, FRM), jnp.int32),
            pltpu.VMEM((2, 2 * N_DP, 256), F32),
            pltpu.VMEM((FRM, 4 * CH), BF16),
            pltpu.VMEM((N_DP, BLK, CH), BF16),
            pltpu.VMEM((N_DP, BLK, CH), BF16),
            pltpu.VMEM((2, UTT, 2 * CH), F32),
            pltpu.VMEM((N_MP, UTT, CH), BF16),
            pltpu.VMEM((N_MP, UTT, CH), BF16),
            pltpu.VMEM((N_MP, RC, CH), F32),
            pltpu.VMEM((NCH, 2 * FC, 2 * C), BF16),
            pltpu.VMEM((NCH, FC, 2 * C), BF16),
            pltpu.VMEM((NCH, 2 * FC, C), F32),
            pltpu.VMEM((NCH, FC, C), F32),
            pltpu.VMEM((NCH, FC, C), BF16),
            pltpu.VMEM((NCH, 2 * FC, C), BF16),
            pltpu.VMEM((N_MP, 4 * UTT, CH), BF16),
            pltpu.VMEM((2, 4, 4, 2, KR, C), F32),
            pltpu.VMEM((2, 4, 4, KR, C), BF16),
            pltpu.VMEM((2, 4, 4, KR, C), BF16),
            pltpu.VMEM((2, 4, 4, KR, C), BF16),
            pltpu.VMEM((2, 4, 4, KR, C), BF16),
            pltpu.VMEM((2, 4, KR, C), F32),
            pltpu.VMEM((2, 4, KR, C), BF16),
            pltpu.VMEM((2, 4, KR, C), BF16),
            pltpu.VMEM((2, KR, C), F32),
            pltpu.VMEM((N_MP, 2, KR, CH), F32),
            pltpu.VMEM((N_MP, 2, KR, CH), F32),
            dma((4,)), dma((4,)), dma((4,)), dma((4,)), dma((4,)), dma((4,)), dma((4,)), dma((4,)),
            dma((2, 4)), dma((2, 4)), dma((2, 4)), dma((2, 4)), dma((2,)), dma((2,)),
            dma((6,)), dma((NCH, N_MP)), dma((NCH, N_MP)), dma((N_DP,)), dma((N_DP,)), dma((N_MP,)), dma((N_MP,)),
            dma((NCH, N_MP)), dma((NCH, N_MP)), dma((2,)), dma((2,)), dma((2, 4)), dma((2, 4)), dma((2, 4)), dma((2, 4)),
            dma((N_MP,)), dma((N_MP,)),
        ],
        compiler_params=pltpu.CompilerParams(
            collective_id=0, has_side_effects=True, vmem_limit_bytes=56 * 2**20,
            fuse_transposed_lhs_in_matmul=True,
        ),
        name="encoder_backward",
    )(features, conv6_weight, conv7_weight, frame_grads, frame_dest, lengths)
    return pl.pallas_call(
        hand_over,
        out_shape=tuple(jax.ShapeDtypeStruct(r.shape, r.dtype) for r in results),
        in_specs=[hbm] * 3,
        out_specs=(hbm,) * 3,
        scratch_shapes=[
            pltpu.VMEM((16 * UTT, CH), BF16), pltpu.VMEM((KR, CH), F32), pltpu.VMEM((KR, CH), F32),
            dma((PARTS + 2,)), dma((PARTS + 2,)),
        ],
        name="hand_over",
    )(*results)


def solution(mesh):
    placed = (P("dp", "mp"), P("dp", "mp"), P("dp", "mp"), P("dp", "mp"), P(), P("dp"))
    return jax.shard_map(
        body,
        mesh=mesh,
        in_specs=placed,
        out_specs=(P("dp", "mp"), P("dp", "mp"), P("dp", "mp")),
        check_vma=False,
    )
```

```python
import jax
import jax.numpy as jnp
from jax import lax
from jax.experimental import pallas as pl
from jax.experimental.pallas import tpu as pltpu
from jax.sharding import PartitionSpec as P

C = 512
FRM = 2048
CAP = 192
N_DP = 32
N_MP = 4
CH = C // N_MP
UTT = FRM // N_MP
FC = 128
NCH = UTT // FC
RC = 4 * FC
PARTS = 8
KR = 32

inv_root_two = 0.7071067811865476
inv_root_tau = 0.3989422804014327
F32 = jnp.float32
BF16 = jnp.bfloat16


def dot(left, right, contract=((1,), (0,))):
    return lax.dot_general(left, right, (contract, ((), ())), preferred_element_type=F32)


def iota(shape, axis):
    return lax.broadcasted_iota(jnp.int32, shape, axis)


def kernel(
    feat, w6, w7, grads_in, dest_in, lens_in,
    gf, g6, g7,
    grads, dest, lens, xin, wts, quad, meta, rhs, obox, arrived, rows_out, rows_in, placed, exb, mg,
    s32, pairs6, pairs7, slope6, slope7, delta7, delta6, gout,
    gsum, core_out, core_in, part_out, part_in, part, chip_out, chip_in, share, x_out, x_in,
    va_s, va_r, vb_s, vb_r, vx_s, vx_r, ux_s, ux_r, ua_s, ua_r, ub_s, ub_r, wc_s, wc_r, own_sem, f_s, f_r, rt_s, rt_r, rn_s, rn_r, ex_s, ex_r,
    go_s, go_r, rc_s, rc_r, ra_s, ra_r, rb_s, rb_r, rx_s, rx_r,
):
    d, m = lax.axis_index("dp"), lax.axis_index("mp")
    z, y, core = lax.div(d, 8), lax.rem(lax.div(d, 2), 4), lax.rem(d, 2)

    def dp_of(dz, dy, dc):
        return lax.rem(z + dz, 4) * 8 + lax.rem(y + dy, 4) * 2 + lax.rem(core + dc, 2)

    def remote(src, dst, send, recv, dp, mp):
        return pltpu.make_async_remote_copy(
            src_ref=src, dst_ref=dst, send_sem=send, recv_sem=recv,
            device_id=(dp, mp), device_id_type=pl.DeviceIdType.MESH,
        )

    barrier = pltpu.get_barrier_semaphore()
    for i in range(1, N_MP):
        pl.semaphore_signal(barrier, inc=1, device_id=(d, lax.rem(m + i, N_MP)), device_id_type=pl.DeviceIdType.MESH)

    @pl.loop(1, N_DP)
    def _(k):
        pl.semaphore_signal(barrier, inc=1, device_id=(lax.rem(d + k, N_DP), m), device_id_type=pl.DeviceIdType.MESH)

    own_rows = pltpu.make_async_copy(
        feat.at[pl.ds(pl.multiple_of(m * 4 * UTT, 4 * UTT), 4 * UTT), :], xin.at[m], own_sem.at[0]
    )
    own_rows.start()
    cols = pl.ds(pl.multiple_of(m * CH, CH), CH)
    local = [
        pltpu.make_async_copy(dest_in.at[pl.ds(pl.multiple_of(d * FRM, FRM), FRM)], dest, own_sem.at[1]),
        pltpu.make_async_copy(grads_in, grads, own_sem.at[2]),
        pltpu.make_async_copy(w6, wts.at[0, z, y, core, :, cols], own_sem.at[3]),
        pltpu.make_async_copy(w7, wts.at[1, z, y, core, :, cols], own_sem.at[4]),
        pltpu.make_async_copy(lens_in, lens, own_sem.at[5]),
    ]
    for copy in local:
        copy.start()
    for copy in local:
        copy.wait()
    pl.semaphore_wait(barrier, N_DP - 1 + N_MP - 1)

    def along_z(i):
        return dp_of(i, 0, 0)

    def along_y(i):
        return dp_of(0, i, 0)

    def va(i):
        block = wts.at[1, z, y, core, :, cols]
        return remote(block, block, va_s.at[i], va_r.at[i], along_y(i), m)

    def vb(i):
        block = wts.at[1, z, :, core, :, cols]
        return remote(block, block, vb_s.at[i], vb_r.at[i], along_z(i), m)

    def vx(i):
        block = wts.at[1, :, :, core, :, cols]
        return remote(block, block, vx_s.at[i], vx_r.at[i], d, lax.rem(m + i, N_MP))

    def ux(i):
        block = wts.at[0, z, y, core, :, cols]
        return remote(block, block, ux_s.at[i], ux_r.at[i], d, lax.rem(m + i, N_MP))

    def ua(h, i):
        block = wts.at[0, z, y, core, :, pl.ds(h * 256, 256)]
        return remote(block, block, ua_s.at[h, i], ua_r.at[h, i], (along_z, along_y)[h](i), m)

    def ub(h, i):
        half = pl.ds(h * 256, 256)
        block = wts.at[0, :, y, core, :, half] if h == 0 else wts.at[0, z, :, core, :, half]
        return remote(block, block, ub_s.at[h, i], ub_r.at[h, i], (along_y, along_z)[h](i), m)

    def wc(w):
        block = wts.at[w, :, :, core]
        return remote(block, block, wc_s.at[w], wc_r.at[w], dp_of(0, 0, 1), m)

    for i in range(1, 4):
        ux(i).start()
        va(i).start()

    def feature(c, i):
        p = lax.rem(m + i, N_MP)
        return remote(
            feat.at[pl.ds(pl.multiple_of(p * 4 * UTT + c * RC, RC), RC), :],
            xin.at[m, pl.ds(pl.multiple_of(c * RC, RC), RC), :],
            f_s.at[c, i], f_r.at[c, i], d, p,
        )

    for c in range(NCH // 2):
        for i in range(1, N_MP):
            feature(c, i).start()

    def number_slots():
        target = dest[...].reshape(1, FRM)
        row = lax.bitwise_and(target, FRM - 1)
        shifted = lambda by, top: lax.bitwise_and(lax.shift_right_logical(target, by), top)
        owner = (
            lax.bitwise_and(shifted(14, 3) - z, 3) * 8
            + lax.bitwise_and(shifted(12, 3) - y, 3) * 2
            + lax.bitwise_and(shifted(11, 1) + core, 1)
        )
        before = jnp.where(iota((256, 256), 0) < iota((256, 256), 1), 1.0, 0.0).astype(BF16)
        carry = jnp.zeros((N_DP, 1), F32)
        ranks = []
        for b in range(FRM // 256):
            mine = owner[:, b * 256 : (b + 1) * 256] == iota((N_DP, 256), 0)
            ones = jnp.where(mine, 1.0, 0.0)
            earlier = dot(ones.astype(BF16), before) + carry
            ranks.append(jnp.sum(jnp.where(mine, earlier, 0.0), axis=0, keepdims=True))
            carry = carry + jnp.sum(ones, axis=1, keepdims=True)
        rank = jnp.concatenate(ranks, axis=1).astype(jnp.int32)
        quad[...] = jnp.where(lax.shift_right_logical(owner, 2) == iota((8, FRM), 0), rank, 4096)
        remainder = jnp.where(lax.bitwise_and(owner, 3) == iota((8, FRM), 0), 1.0, 0.0).astype(BF16)
        spread = jnp.where(iota((8, 4 * CH), 0) == lax.div(iota((8, 4 * CH), 1), CH), 1.0, 0.0).astype(BF16)
        for b in range(FRM // 256):
            part_ = slice(b * 256, (b + 1) * 256)
            keep = dot(remainder[:, part_], spread, ((0,), (0,))).astype(BF16)
            rows = grads[part_, :]
            rhs[part_, :] = keep * jnp.concatenate([rows] * 4, axis=1)
        line = iota((2 * N_DP, FRM), 0)
        digits = jnp.where(
            line == owner, lax.shift_right_logical(row, 8),
            jnp.where(line == owner + N_DP, lax.bitwise_and(row, 255), 0),
        ).astype(F32).astype(BF16)
        for odd in range(2):
            pick = jnp.where(iota((256, FRM), 0) == rank + 64 * odd, 1.0, 0.0).astype(BF16)
            meta[odd] = dot(digits, pick, ((1,), (1,)))

    number_slots()
    for i in range(1, 4):
        va(i).wait()
        ux(i).wait()
    for i in range(1, 4):
        vb(i).start()
        ua(0, i).start()
        ua(1, i).start()

    def routed(k):
        return remote(
            obox.at[k], arrived.at[k], rt_s.at[k], rt_r.at[k],
            dp_of(lax.div(k, 8), lax.rem(lax.div(k, 2), 4), lax.rem(k, 2)), m,
        )

    def numbers(k):
        return remote(
            rows_out.at[k], rows_in.at[k], rn_s.at[k], rn_r.at[k],
            dp_of(lax.div(k, 8), lax.rem(lax.div(k, 2), 4), lax.rem(k, 2)), m,
        )

    own_numbers = pltpu.make_async_copy(rows_out.at[0], rows_in.at[0], rn_r.at[0])
    own_block = pltpu.make_async_copy(obox.at[0], arrived.at[0], rt_r.at[0])

    def pack(g):
        pick = jnp.where(iota((CAP, FRM), 0) == quad[pl.ds(g, 1), :], 1.0, 0.0).astype(BF16)
        both = dot(pick, rhs[...])
        for j in range(4):
            k = g * 4 + j
            obox[k] = both[:, j * CH : (j + 1) * CH].astype(BF16)
            high, low = meta[j % 2, pl.ds(k, 1), :], meta[j % 2, pl.ds(k + N_DP, 1), :]
            rows = high * 256.0 + low
            rows_out[k, 0:1, :] = rows[:, :128]
            rows_out[k, 1:2, :] = rows[:, 128:]

    @pl.loop(0, 8)
    def _(i):
        g = lax.rem(5 * i + 2, 8)
        pack(g)
        for j in range(1, 4):
            numbers(g * 4 + j).start()
            routed(g * 4 + j).start()

        @pl.when(g != 0)
        def _():
            numbers(g * 4).start()
            routed(g * 4).start()

        @pl.when(g == 0)
        def _():
            own_numbers.start()
            own_block.start()

    for i in range(1, 4):
        vb(i).wait()
        ua(0, i).wait()
        ua(1, i).wait()
    for i in range(1, 4):
        vx(i).start()
    for c in range(NCH // 2, NCH):
        for i in range(1, N_MP):
            feature(c, i).start()

    def place(g):
        first, second = [], []
        for i in range(4):
            first.append(rows_in[g * 4 + i, 0:1, :])
            second.append(rows_in[g * 4 + i, 1:2, :])
        left = iota((1, 128), 1) < 64
        at = jnp.concatenate(
            [
                first[0], jnp.where(left, second[0], first[1]), second[1],
                first[2], jnp.where(left, second[2], first[3]), second[3],
            ],
            axis=1,
        ).astype(jnp.int32)
        half = lax.shift_right_logical(at, 10)
        within = lax.bitwise_and(at, 1023)
        top = jnp.where(iota((8, 4 * CAP), 0) == 0, half, 0).astype(F32).astype(BF16)
        later = dot(top, jnp.ones((8, CH), BF16), ((0,), (0,))).astype(BF16)
        block = arrived[pl.ds(g * 4, 4)].reshape(4 * CAP, CH)
        second_half = block * later
        sides = jnp.concatenate([block - second_half, second_half], axis=1)
        for a in range(2):
            pick = jnp.where(iota((UTT, 4 * CAP), 0) + a * UTT == within, 1.0, 0.0).astype(BF16)
            placed[a] += dot(pick, sides)

    placed[...] = jnp.zeros((2, UTT, 2 * CH), F32)

    @pl.loop(0, 8)
    def _(i):
        g = lax.rem(5 * i + 2, 8)
        for j in range(1, 4):
            numbers(g * 4 + j).wait()
            routed(g * 4 + j).wait()

        @pl.when(g != 0)
        def _():
            numbers(g * 4).wait()
            routed(g * 4).wait()

        @pl.when(g == 0)
        def _():
            own_numbers.wait()
            own_block.wait()

        place(g)

        @pl.when(i == 3)
        def _():
            for n in range(1, 4):
                ub(0, n).start()
                ub(1, n).start()

    def exchange(i):
        p = lax.rem(m + i, N_MP)
        return remote(exb.at[p], mg.at[m], ex_s.at[i], ex_r.at[i], d, p)

    for p in range(N_MP):
        exb[p] = placed[p % 2, :, (p // 2) * CH : (p // 2 + 1) * CH].astype(BF16)
    for i in range(1, N_MP):
        exchange(i).start()
    mg[m] = exb[m]

    for i in range(1, 4):
        ub(0, i).wait()
        ub(1, i).wait()
    wc(0).start()
    for i in range(1, 4):
        vx(i).wait()
    wc(1).start()
    own_rows.wait()

    def unpair(c):
        rows = pl.ds(pl.multiple_of(c * RC, RC), RC)
        for g in range(N_MP):
            s32[g] = xin[g, rows, :].astype(F32)
        for j in range(4):
            for g in range(N_MP):
                lanes = slice((j % 2) * C + g * CH, (j % 2) * C + (g + 1) * CH)
                pairs6[c, (j // 2) * FC : (j // 2 + 1) * FC, lanes] = s32[g, pl.ds(j, FC, stride=4), :].astype(BF16)

    def forward(c):
        pre = dot(pairs6[c], wts[0].reshape(2 * C, C))
        half = 0.5 * (1.0 + lax.erf(pre * inv_root_two))
        act = (pre * half).astype(BF16)
        slope6[c] = half + pre * jnp.exp(-0.5 * pre * pre) * inv_root_tau
        pairs7[c, :, 0:C] = act[:FC]
        pairs7[c, :, C : 2 * C] = act[FC:]
        pre = dot(pairs7[c], wts[1].reshape(2 * C, C))
        half = 0.5 * (1.0 + lax.erf(pre * inv_root_two))
        slope7[c] = half + pre * jnp.exp(-0.5 * pre * pre) * inv_root_tau

    for c in range(NCH):
        for i in range(1, N_MP):
            feature(c, i).wait()
        unpair(c)
    for w in range(2):
        wc(w).wait()
    for c in range(NCH):
        forward(c)

    for i in range(1, N_MP):
        exchange(i).wait()

    valid = lax.div(lens[m] - 400, 320) + 1

    def given(c, i):
        p = lax.rem(m + i, N_MP)
        return remote(
            gout.at[p, pl.ds(pl.multiple_of(c * RC, RC), RC), :],
            gf.at[pl.ds(pl.multiple_of(m * 4 * UTT + c * RC, RC), RC), :],
            go_s.at[c, i], go_r.at[c, i], d, p,
        )

    def own_given(c):
        return pltpu.make_async_copy(
            gout.at[m, pl.ds(pl.multiple_of(c * RC, RC), RC), :],
            gf.at[pl.ds(pl.multiple_of(m * 4 * UTT + c * RC, RC), RC), :],
            go_s.at[c, 0],
        )

    def backward(c):
        frames = pl.ds(pl.multiple_of(c * FC, FC), FC)
        live = iota((FC, CH), 0) + c * FC < valid
        for g in range(N_MP):
            lanes = slice(g * CH, (g + 1) * CH)
            coming = jnp.where(live, mg[g, frames, :].astype(F32), 0.0)
            delta7[c, :, lanes] = (coming * slope7[c, :, lanes]).astype(BF16)
        back = dot(delta7[c], wts[1].reshape(2 * C, C), ((1,), (1,)))
        delta6[c, 0:FC, :] = (back[:, :C] * slope6[c, 0:FC, :]).astype(BF16)
        delta6[c, FC : 2 * FC, :] = (back[:, C:] * slope6[c, FC : 2 * FC, :]).astype(BF16)
        back = dot(delta6[c], wts[0].reshape(2 * C, C), ((1,), (1,)))
        for j in range(4):
            for g in range(N_MP):
                s32[g, pl.ds(j, FC, stride=4), :] = back[
                    (j // 2) * FC : (j // 2 + 1) * FC, (j % 2) * C + g * CH : (j % 2) * C + (g + 1) * CH
                ]
        for g in range(N_MP):
            gout[g, pl.ds(pl.multiple_of(c * RC, RC), RC), :] = s32[g].astype(BF16)

    @pl.loop(0, NCH)
    def _(c):
        backward(c)
        for i in range(1, N_MP):
            given(c, i).start()
        own_given(c).start()

    def terms(w, b):
        pairs, deltas, count = ((pairs6, delta6, 2 * UTT), (pairs7, delta7, UTT))[w]
        left = pairs[:, :, pl.ds(pl.multiple_of(b * 256, 256), 256)].reshape(count, 256)
        right = deltas[...].reshape(count, C)
        gsum[w, b] = dot(left, right, ((0,), (0,))).reshape(4, 2, KR, C)

    def to_mate(w):
        return remote(core_out.at[w], core_in.at[w], rc_s.at[w], rc_r.at[w], dp_of(0, 0, 1), m)

    def ra(w, i):
        p = lax.rem((z, y)[w] + i, 4)
        return remote(
            part_out.at[w, p], part_in.at[w, i], ra_s.at[w, i], ra_r.at[w, i], (along_z, along_y)[w](i), m
        )

    def rb(w, i):
        p = lax.rem((y, z)[w] + i, 4)
        return remote(
            chip_out.at[w, p], chip_in.at[w, i], rb_s.at[w, i], rb_r.at[w, i], (along_y, along_z)[w](i), m
        )

    for w in (1, 0):

        @pl.loop(0, 4)
        def _(b):
            terms(w, b)
            core_out[w, b] = gsum[w, b, :, 1 - core].astype(BF16)

        to_mate(w).start()

    for w in (1, 0):
        to_mate(w).wait()

        @pl.loop(0, 4)
        def _(a):
            for b in range(4):
                zy = (a, b) if w == 0 else (b, a)
                total = gsum[w, zy[0], zy[1], core] + core_in[w, zy[0], zy[1]].astype(F32)
                part_out[w, a, b] = total.astype(BF16)

        for i in range(1, 4):
            ra(w, i).start()

    for w in (1, 0):
        for b in range(4):
            zy = (z, b) if w == 0 else (b, y)
            part[w, b] = gsum[w, zy[0], zy[1], core] + core_in[w, zy[0], zy[1]].astype(F32)
        for i in range(1, 4):
            ra(w, i).wait()
            part[w] += part_in[w, i].astype(F32)
        chip_out[w] = part[w].astype(BF16)
        for i in range(1, 4):
            rb(w, i).start()

    for w in (1, 0):
        share[w] = part[w, (y, z)[w]]
        for i in range(1, 4):
            rb(w, i).wait()
            share[w] += chip_in[w, i].astype(F32)
    for g in range(N_MP):
        x_out[g] = share[:, :, g * CH : (g + 1) * CH]

    def along(i):
        p = lax.rem(m + i, N_MP)
        return remote(x_out.at[p], x_in.at[i], rx_s.at[i], rx_r.at[i], d, p)

    for i in range(1, N_MP):
        along(i).start()
    total = x_out[m]
    for i in range(1, N_MP):
        along(i).wait()
        total = total + x_in[i]
    g6[...] = total[0]
    g7[...] = total[1]

    @pl.loop(0, NCH)
    def _(c):
        for i in range(1, N_MP):
            given(c, i).wait()
        own_given(c).wait()


def hand_over(gf, g6, g7, gf_out, g6_out, g7_out, held, held6, held7, sem_in, sem_out):
    steps = [(g6, held6, g6_out), (g7, held7, g7_out)]
    for p in range(PARTS):
        rows = pl.ds(p * (16 * UTT // PARTS), 16 * UTT // PARTS)
        steps.append((gf.at[rows], held.at[rows], gf_out.at[rows]))
    come = [pltpu.make_async_copy(a, b, sem_in.at[n]) for n, (a, b, _) in enumerate(steps)]
    go = [pltpu.make_async_copy(b, c, sem_out.at[n]) for n, (_, b, c) in enumerate(steps)]
    for copy in come:
        copy.start()
    for here, there in zip(come, go):
        here.wait()
        there.start()
    for copy in go:
        copy.wait()


def body(features, conv6_weight, conv7_weight, frame_grads, frame_dest, lengths):
    vmem, hbm = pl.BlockSpec(memory_space=pltpu.VMEM), pl.BlockSpec(memory_space=pl.ANY)
    dma = pltpu.SemaphoreType.DMA
    results = pl.pallas_call(
        kernel,
        out_shape=(
            jax.ShapeDtypeStruct(features.shape, BF16),
            jax.ShapeDtypeStruct(conv6_weight.shape, F32),
            jax.ShapeDtypeStruct(conv7_weight.shape, F32),
        ),
        in_specs=[hbm] * 6,
        out_specs=(hbm, vmem, vmem),
        scratch_shapes=[
            pltpu.VMEM((FRM, CH), BF16),
            pltpu.VMEM((FRM,), jnp.int32),
            pltpu.SMEM((N_MP,), jnp.int32),
            pltpu.VMEM((N_MP, 4 * UTT, CH), BF16),
            pltpu.VMEM((2, 4, 4, 2, KR, C), BF16),
            pltpu.VMEM((8, FRM), jnp.int32),
            pltpu.VMEM((2, 2 * N_DP, 256), F32),
            pltpu.VMEM((FRM, 4 * CH), BF16),
            pltpu.VMEM((N_DP, CAP, CH), BF16),
            pltpu.VMEM((N_DP, CAP, CH), BF16),
            pltpu.VMEM((N_DP, 2, 128), F32),
            pltpu.VMEM((N_DP, 2, 128), F32),
            pltpu.VMEM((2, UTT, 2 * CH), F32),
            pltpu.VMEM((N_MP, UTT, CH), BF16),
            pltpu.VMEM((N_MP, UTT, CH), BF16),
            pltpu.VMEM((N_MP, RC, CH), F32),
            pltpu.VMEM((NCH, 2 * FC, 2 * C), BF16),
            pltpu.VMEM((NCH, FC, 2 * C), BF16),
            pltpu.VMEM((NCH, 2 * FC, C), F32),
            pltpu.VMEM((NCH, FC, C), F32),
            pltpu.VMEM((NCH, FC, C), BF16),
            pltpu.VMEM((NCH, 2 * FC, C), BF16),
            pltpu.VMEM((N_MP, 4 * UTT, CH), BF16),
            pltpu.VMEM((2, 4, 4, 2, KR, C), F32),
            pltpu.VMEM((2, 4, 4, KR, C), BF16),
            pltpu.VMEM((2, 4, 4, KR, C), BF16),
            pltpu.VMEM((2, 4, 4, KR, C), BF16),
            pltpu.VMEM((2, 4, 4, KR, C), BF16),
            pltpu.VMEM((2, 4, KR, C), F32),
            pltpu.VMEM((2, 4, KR, C), BF16),
            pltpu.VMEM((2, 4, KR, C), BF16),
            pltpu.VMEM((2, KR, C), F32),
            pltpu.VMEM((N_MP, 2, KR, CH), F32),
            pltpu.VMEM((N_MP, 2, KR, CH), F32),
            dma((4,)), dma((4,)), dma((4,)), dma((4,)), dma((4,)), dma((4,)), dma((4,)), dma((4,)),
            dma((2, 4)), dma((2, 4)), dma((2, 4)), dma((2, 4)), dma((2,)), dma((2,)),
            dma((6,)), dma((NCH, N_MP)), dma((NCH, N_MP)), dma((N_DP,)), dma((N_DP,)), dma((N_DP,)), dma((N_DP,)), dma((N_MP,)), dma((N_MP,)),
            dma((NCH, N_MP)), dma((NCH, N_MP)), dma((2,)), dma((2,)), dma((2, 4)), dma((2, 4)), dma((2, 4)), dma((2, 4)),
            dma((N_MP,)), dma((N_MP,)),
        ],
        compiler_params=pltpu.CompilerParams(
            collective_id=0, has_side_effects=True, vmem_limit_bytes=56 * 2**20,
            fuse_transposed_lhs_in_matmul=True,
        ),
        name="encoder_backward",
    )(features, conv6_weight, conv7_weight, frame_grads, frame_dest, lengths)
    return pl.pallas_call(
        hand_over,
        out_shape=tuple(jax.ShapeDtypeStruct(r.shape, r.dtype) for r in results),
        in_specs=[hbm] * 3,
        out_specs=(hbm,) * 3,
        scratch_shapes=[
            pltpu.VMEM((16 * UTT, CH), BF16), pltpu.VMEM((KR, CH), F32), pltpu.VMEM((KR, CH), F32),
            dma((PARTS + 2,)), dma((PARTS + 2,)),
        ],
        name="hand_over",
    )(*results)


def solution(mesh):
    placed = (P("dp", "mp"), P("dp", "mp"), P("dp", "mp"), P("dp", "mp"), P(), P("dp"))
    return jax.shard_map(
        body,
        mesh=mesh,
        in_specs=placed,
        out_specs=(P("dp", "mp"), P("dp", "mp"), P("dp", "mp")),
        check_vma=False,
    )
```

```python
import jax
import jax.numpy as jnp
from jax import lax
from jax.experimental import pallas as pl
from jax.experimental.pallas import tpu as pltpu
from jax.sharding import PartitionSpec as P

C = 512
FRM = 2048
CAP = 192
N_DP = 32
N_MP = 4
CH = C // N_MP
UTT = FRM // N_MP
FC = 128
NCH = UTT // FC
RC = 4 * FC
PARTS = 8
META = 16
BLK = CAP + META
KR = 32

inv_root_two = 0.7071067811865476
inv_root_tau = 0.3989422804014327
F32 = jnp.float32
BF16 = jnp.bfloat16


def dot(left, right, contract=((1,), (0,))):
    return lax.dot_general(left, right, (contract, ((), ())), preferred_element_type=F32)


def iota(shape, axis):
    return lax.broadcasted_iota(jnp.int32, shape, axis)


def kernel(
    feat, w6, w7, grads_in, dest_in, lens_in,
    gf, g6, g7,
    grads, dest, lens, xin, wts, quad, meta, rhs, obox, arrived, placed, exb, mg,
    s32, pairs6, pairs7, slope6, slope7, delta7, delta6, gout,
    gsum, core_out, core_in, part_out, part_in, part, chip_out, chip_in, share, x_out, x_in,
    va_s, va_r, vb_s, vb_r, vx_s, vx_r, ux_s, ux_r, ua_s, ua_r, ub_s, ub_r, wc_s, wc_r, own_sem, f_s, f_r, rt_s, rt_r, ex_s, ex_r,
    go_s, go_r, rc_s, rc_r, ra_s, ra_r, rb_s, rb_r, rx_s, rx_r,
):
    d, m = lax.axis_index("dp"), lax.axis_index("mp")
    z, y, core = lax.div(d, 8), lax.rem(lax.div(d, 2), 4), lax.rem(d, 2)

    def dp_of(dz, dy, dc):
        return lax.rem(z + dz, 4) * 8 + lax.rem(y + dy, 4) * 2 + lax.rem(core + dc, 2)

    def remote(src, dst, send, recv, dp, mp):
        return pltpu.make_async_remote_copy(
            src_ref=src, dst_ref=dst, send_sem=send, recv_sem=recv,
            device_id=(dp, mp), device_id_type=pl.DeviceIdType.MESH,
        )

    barrier = pltpu.get_barrier_semaphore()
    for i in range(1, N_MP):
        pl.semaphore_signal(barrier, inc=1, device_id=(d, lax.rem(m + i, N_MP)), device_id_type=pl.DeviceIdType.MESH)

    @pl.loop(1, N_DP)
    def _(k):
        pl.semaphore_signal(barrier, inc=1, device_id=(lax.rem(d + k, N_DP), m), device_id_type=pl.DeviceIdType.MESH)

    own_rows = pltpu.make_async_copy(
        feat.at[pl.ds(pl.multiple_of(m * 4 * UTT, 4 * UTT), 4 * UTT), :], xin.at[m], own_sem.at[0]
    )
    own_rows.start()
    cols = pl.ds(pl.multiple_of(m * CH, CH), CH)
    local = [
        pltpu.make_async_copy(dest_in.at[pl.ds(pl.multiple_of(d * FRM, FRM), FRM)], dest, own_sem.at[1]),
        pltpu.make_async_copy(grads_in, grads, own_sem.at[2]),
        pltpu.make_async_copy(w6, wts.at[0, z, y, core, :, cols], own_sem.at[3]),
        pltpu.make_async_copy(w7, wts.at[1, z, y, core, :, cols], own_sem.at[4]),
        pltpu.make_async_copy(lens_in, lens, own_sem.at[5]),
    ]
    for copy in local:
        copy.start()
    for copy in local:
        copy.wait()
    pl.semaphore_wait(barrier, N_DP - 1 + N_MP - 1)

    def along_z(i):
        return dp_of(i, 0, 0)

    def along_y(i):
        return dp_of(0, i, 0)

    def va(i):
        block = wts.at[1, z, y, core, :, cols]
        return remote(block, block, va_s.at[i], va_r.at[i], along_y(i), m)

    def vb(i):
        block = wts.at[1, z, :, core, :, cols]
        return remote(block, block, vb_s.at[i], vb_r.at[i], along_z(i), m)

    def vx(i):
        block = wts.at[1, :, :, core, :, cols]
        return remote(block, block, vx_s.at[i], vx_r.at[i], d, lax.rem(m + i, N_MP))

    def ux(i):
        block = wts.at[0, z, y, core, :, cols]
        return remote(block, block, ux_s.at[i], ux_r.at[i], d, lax.rem(m + i, N_MP))

    def ua(h, i):
        block = wts.at[0, z, y, core, :, pl.ds(h * 256, 256)]
        return remote(block, block, ua_s.at[h, i], ua_r.at[h, i], (along_z, along_y)[h](i), m)

    def ub(h, i):
        half = pl.ds(h * 256, 256)
        block = wts.at[0, :, y, core, :, half] if h == 0 else wts.at[0, z, :, core, :, half]
        return remote(block, block, ub_s.at[h, i], ub_r.at[h, i], (along_y, along_z)[h](i), m)

    def wc(w):
        block = wts.at[w, :, :, core]
        return remote(block, block, wc_s.at[w], wc_r.at[w], dp_of(0, 0, 1), m)

    for i in range(1, 4):
        ux(i).start()
        va(i).start()

    def feature(c, i):
        p = lax.rem(m + i, N_MP)
        return remote(
            feat.at[pl.ds(pl.multiple_of(p * 4 * UTT + c * RC, RC), RC), :],
            xin.at[m, pl.ds(pl.multiple_of(c * RC, RC), RC), :],
            f_s.at[c, i], f_r.at[c, i], d, p,
        )

    for c in range(NCH // 2):
        for i in range(1, N_MP):
            feature(c, i).start()

    def number_slots():
        target = dest[...].reshape(1, FRM)
        row = lax.bitwise_and(target, FRM - 1)
        shifted = lambda by, top: lax.bitwise_and(lax.shift_right_logical(target, by), top)
        owner = (
            lax.bitwise_and(shifted(14, 3) - z, 3) * 8
            + lax.bitwise_and(shifted(12, 3) - y, 3) * 2
            + lax.bitwise_and(shifted(11, 1) + core, 1)
        )
        before = jnp.where(iota((256, 256), 0) < iota((256, 256), 1), 1.0, 0.0).astype(BF16)
        carry = jnp.zeros((N_DP, 1), F32)
        ranks = []
        for b in range(FRM // 256):
            mine = owner[:, b * 256 : (b + 1) * 256] == iota((N_DP, 256), 0)
            ones = jnp.where(mine, 1.0, 0.0)
            earlier = dot(ones.astype(BF16), before) + carry
            ranks.append(jnp.sum(jnp.where(mine, earlier, 0.0), axis=0, keepdims=True))
            carry = carry + jnp.sum(ones, axis=1, keepdims=True)
        rank = jnp.concatenate(ranks, axis=1).astype(jnp.int32)
        quad[...] = jnp.where(lax.shift_right_logical(owner, 2) == iota((8, FRM), 0), rank, 4096)
        remainder = jnp.where(lax.bitwise_and(owner, 3) == iota((8, FRM), 0), 1.0, 0.0).astype(BF16)
        spread = jnp.where(iota((8, 4 * CH), 0) == lax.div(iota((8, 4 * CH), 1), CH), 1.0, 0.0).astype(BF16)
        for b in range(FRM // 256):
            part_ = slice(b * 256, (b + 1) * 256)
            keep = dot(remainder[:, part_], spread, ((0,), (0,))).astype(BF16)
            rows = grads[part_, :]
            rhs[part_, :] = keep * jnp.concatenate([rows] * 4, axis=1)
        line = iota((2 * N_DP, FRM), 0)
        digits = jnp.where(
            line == owner, lax.shift_right_logical(row, 8),
            jnp.where(line == owner + N_DP, lax.bitwise_and(row, 255), 0),
        ).astype(F32).astype(BF16)
        for odd in range(2):
            pick = jnp.where(iota((256, FRM), 0) == rank + 64 * odd, 1.0, 0.0).astype(BF16)
            meta[odd] = dot(digits, pick, ((1,), (1,)))

    number_slots()
    def routed(k):
        return remote(
            obox.at[k], arrived.at[k], rt_s.at[k], rt_r.at[k],
            dp_of(lax.div(k, 8), lax.rem(lax.div(k, 2), 4), lax.rem(k, 2)), m,
        )

    own_block = pltpu.make_async_copy(obox.at[0], arrived.at[0], rt_r.at[0])

    def pack(g):
        pick = jnp.where(iota((CAP, FRM), 0) == quad[pl.ds(g, 1), :], 1.0, 0.0).astype(BF16)
        both = dot(pick, rhs[...])
        line = iota((META, 128), 0)
        for j in range(4):
            k = g * 4 + j
            obox[k, 0:CAP, :] = both[:, j * CH : (j + 1) * CH].astype(BF16)
            high, low = meta[j % 2, pl.ds(k, 1), :], meta[j % 2, pl.ds(k + N_DP, 1), :]
            tile = jnp.where(line == 0, high[:, :128], jnp.where(line == 1, high[:, 128:], 0.0))
            tile = jnp.where(line == 2, low[:, :128], jnp.where(line == 3, low[:, 128:], tile))
            obox[k, CAP:BLK, :] = tile.astype(BF16)

    @pl.loop(0, 8)
    def _(i):
        g = lax.rem(5 * i + 2, 8)
        pack(g)
        for j in range(1, 4):
            routed(g * 4 + j).start()

        @pl.when(g != 0)
        def _():
            routed(g * 4).start()

        @pl.when(g == 0)
        def _():
            own_block.start()

        @pl.when(i == 0)
        def _():
            for n in range(1, 4):
                va(n).wait()
                ux(n).wait()
            for n in range(1, 4):
                vb(n).start()
                ua(0, n).start()
                ua(1, n).start()

    for i in range(1, 4):
        vb(i).wait()
        ua(0, i).wait()
        ua(1, i).wait()
    for i in range(1, 4):
        vx(i).start()
    for c in range(NCH // 2, NCH):
        for i in range(1, N_MP):
            feature(c, i).start()

    def place(g):
        first, second = [], []
        for i in range(4):
            digits = arrived[g * 4 + i, CAP:BLK, :].astype(F32)
            first.append(digits[0:1] * 256.0 + digits[2:3])
            second.append(digits[1:2] * 256.0 + digits[3:4])
        left = iota((1, 128), 1) < 64
        at = jnp.concatenate(
            [
                first[0], jnp.where(left, second[0], first[1]), second[1],
                first[2], jnp.where(left, second[2], first[3]), second[3],
            ],
            axis=1,
        ).astype(jnp.int32)
        half = lax.shift_right_logical(at, 10)
        within = lax.bitwise_and(at, 1023)
        top = jnp.where(iota((8, 4 * CAP), 0) == 0, half, 0).astype(F32).astype(BF16)
        later = dot(top, jnp.ones((8, CH), BF16), ((0,), (0,))).astype(BF16)
        block = arrived[pl.ds(g * 4, 4), 0:CAP, :].reshape(4 * CAP, CH)
        second_half = block * later
        sides = jnp.concatenate([block - second_half, second_half], axis=1)
        for a in range(2):
            pick = jnp.where(iota((UTT, 4 * CAP), 0) + a * UTT == within, 1.0, 0.0).astype(BF16)
            placed[a] += dot(pick, sides)

    placed[...] = jnp.zeros((2, UTT, 2 * CH), F32)

    @pl.loop(0, 8)
    def _(i):
        g = lax.rem(5 * i + 2, 8)
        for j in range(1, 4):
            routed(g * 4 + j).wait()

        @pl.when(g != 0)
        def _():
            routed(g * 4).wait()

        @pl.when(g == 0)
        def _():
            own_block.wait()

        place(g)

        @pl.when(i == 3)
        def _():
            for n in range(1, 4):
                ub(0, n).start()
                ub(1, n).start()

    def exchange(i):
        p = lax.rem(m + i, N_MP)
        return remote(exb.at[p], mg.at[m], ex_s.at[i], ex_r.at[i], d, p)

    for p in range(N_MP):
        exb[p] = placed[p % 2, :, (p // 2) * CH : (p // 2 + 1) * CH].astype(BF16)
    for i in range(1, N_MP):
        exchange(i).start()
    mg[m] = exb[m]

    for i in range(1, 4):
        ub(0, i).wait()
        ub(1, i).wait()
    wc(0).start()
    for i in range(1, 4):
        vx(i).wait()
    wc(1).start()
    own_rows.wait()

    def unpair(c):
        rows = pl.ds(pl.multiple_of(c * RC, RC), RC)
        for g in range(N_MP):
            s32[g] = xin[g, rows, :].astype(F32)
        for j in range(4):
            for g in range(N_MP):
                lanes = slice((j % 2) * C + g * CH, (j % 2) * C + (g + 1) * CH)
                pairs6[c, (j // 2) * FC : (j // 2 + 1) * FC, lanes] = s32[g, pl.ds(j, FC, stride=4), :].astype(BF16)

    def forward(c):
        pre = dot(pairs6[c], wts[0].reshape(2 * C, C))
        half = 0.5 * (1.0 + lax.erf(pre * inv_root_two))
        act = (pre * half).astype(BF16)
        slope6[c] = half + pre * jnp.exp(-0.5 * pre * pre) * inv_root_tau
        pairs7[c, :, 0:C] = act[:FC]
        pairs7[c, :, C : 2 * C] = act[FC:]
        pre = dot(pairs7[c], wts[1].reshape(2 * C, C))
        half = 0.5 * (1.0 + lax.erf(pre * inv_root_two))
        slope7[c] = half + pre * jnp.exp(-0.5 * pre * pre) * inv_root_tau

    for c in range(NCH):
        for i in range(1, N_MP):
            feature(c, i).wait()
        unpair(c)
    for w in range(2):
        wc(w).wait()
    for c in range(NCH):
        forward(c)

    for i in range(1, N_MP):
        exchange(i).wait()

    valid = lax.div(lens[m] - 400, 320) + 1

    def given(c, i):
        p = lax.rem(m + i, N_MP)
        return remote(
            gout.at[p, pl.ds(pl.multiple_of(c * RC, RC), RC), :],
            gf.at[pl.ds(pl.multiple_of(m * 4 * UTT + c * RC, RC), RC), :],
            go_s.at[c, i], go_r.at[c, i], d, p,
        )

    def own_given(c):
        return pltpu.make_async_copy(
            gout.at[m, pl.ds(pl.multiple_of(c * RC, RC), RC), :],
            gf.at[pl.ds(pl.multiple_of(m * 4 * UTT + c * RC, RC), RC), :],
            go_s.at[c, 0],
        )

    def backward(c):
        frames = pl.ds(pl.multiple_of(c * FC, FC), FC)
        live = iota((FC, CH), 0) + c * FC < valid
        for g in range(N_MP):
            lanes = slice(g * CH, (g + 1) * CH)
            coming = jnp.where(live, mg[g, frames, :].astype(F32), 0.0)
            delta7[c, :, lanes] = (coming * slope7[c, :, lanes]).astype(BF16)
        back = dot(delta7[c], wts[1].reshape(2 * C, C), ((1,), (1,)))
        delta6[c, 0:FC, :] = (back[:, :C] * slope6[c, 0:FC, :]).astype(BF16)
        delta6[c, FC : 2 * FC, :] = (back[:, C:] * slope6[c, FC : 2 * FC, :]).astype(BF16)
        back = dot(delta6[c], wts[0].reshape(2 * C, C), ((1,), (1,)))
        for j in range(4):
            for g in range(N_MP):
                s32[g, pl.ds(j, FC, stride=4), :] = back[
                    (j // 2) * FC : (j // 2 + 1) * FC, (j % 2) * C + g * CH : (j % 2) * C + (g + 1) * CH
                ]
        for g in range(N_MP):
            gout[g, pl.ds(pl.multiple_of(c * RC, RC), RC), :] = s32[g].astype(BF16)

    @pl.loop(0, NCH)
    def _(c):
        backward(c)
        for i in range(1, N_MP):
            given(c, i).start()
        own_given(c).start()

    def terms(w, b):
        pairs, deltas, count = ((pairs6, delta6, 2 * UTT), (pairs7, delta7, UTT))[w]
        left = pairs[:, :, pl.ds(pl.multiple_of(b * 256, 256), 256)].reshape(count, 256)
        right = deltas[...].reshape(count, C)
        gsum[w, b] = dot(left, right, ((0,), (0,))).reshape(4, 2, KR, C)

    def to_mate(w):
        return remote(core_out.at[w], core_in.at[w], rc_s.at[w], rc_r.at[w], dp_of(0, 0, 1), m)

    def ra(w, i):
        p = lax.rem((z, y)[w] + i, 4)
        return remote(
            part_out.at[w, p], part_in.at[w, i], ra_s.at[w, i], ra_r.at[w, i], (along_z, along_y)[w](i), m
        )

    def rb(w, i):
        p = lax.rem((y, z)[w] + i, 4)
        return remote(
            chip_out.at[w, p], chip_in.at[w, i], rb_s.at[w, i], rb_r.at[w, i], (along_y, along_z)[w](i), m
        )

    for w in (1, 0):

        @pl.loop(0, 4)
        def _(b):
            terms(w, b)
            core_out[w, b] = gsum[w, b, :, 1 - core].astype(BF16)

        to_mate(w).start()

    for w in (1, 0):
        to_mate(w).wait()

        @pl.loop(0, 4)
        def _(a):
            for b in range(4):
                zy = (a, b) if w == 0 else (b, a)
                total = gsum[w, zy[0], zy[1], core] + core_in[w, zy[0], zy[1]].astype(F32)
                part_out[w, a, b] = total.astype(BF16)

        for i in range(1, 4):
            ra(w, i).start()

    for w in (1, 0):
        for b in range(4):
            zy = (z, b) if w == 0 else (b, y)
            part[w, b] = gsum[w, zy[0], zy[1], core] + core_in[w, zy[0], zy[1]].astype(F32)
        for i in range(1, 4):
            ra(w, i).wait()
            part[w] += part_in[w, i].astype(F32)
        chip_out[w] = part[w].astype(BF16)
        for i in range(1, 4):
            rb(w, i).start()

    for w in (1, 0):
        share[w] = part[w, (y, z)[w]]
        for i in range(1, 4):
            rb(w, i).wait()
            share[w] += chip_in[w, i].astype(F32)
    for g in range(N_MP):
        x_out[g] = share[:, :, g * CH : (g + 1) * CH]

    def along(i):
        p = lax.rem(m + i, N_MP)
        return remote(x_out.at[p], x_in.at[i], rx_s.at[i], rx_r.at[i], d, p)

    for i in range(1, N_MP):
        along(i).start()
    total = x_out[m]
    for i in range(1, N_MP):
        along(i).wait()
        total = total + x_in[i]
    g6[...] = total[0]
    g7[...] = total[1]

    @pl.loop(0, NCH)
    def _(c):
        for i in range(1, N_MP):
            given(c, i).wait()
        own_given(c).wait()


def hand_over(gf, g6, g7, gf_out, g6_out, g7_out, held, held6, held7, sem_in, sem_out):
    steps = [(g6, held6, g6_out), (g7, held7, g7_out)]
    for p in range(PARTS):
        rows = pl.ds(p * (16 * UTT // PARTS), 16 * UTT // PARTS)
        steps.append((gf.at[rows], held.at[rows], gf_out.at[rows]))
    come = [pltpu.make_async_copy(a, b, sem_in.at[n]) for n, (a, b, _) in enumerate(steps)]
    go = [pltpu.make_async_copy(b, c, sem_out.at[n]) for n, (_, b, c) in enumerate(steps)]
    for copy in come:
        copy.start()
    for here, there in zip(come, go):
        here.wait()
        there.start()
    for copy in go:
        copy.wait()


def body(features, conv6_weight, conv7_weight, frame_grads, frame_dest, lengths):
    vmem, hbm = pl.BlockSpec(memory_space=pltpu.VMEM), pl.BlockSpec(memory_space=pl.ANY)
    dma = pltpu.SemaphoreType.DMA
    results = pl.pallas_call(
        kernel,
        out_shape=(
            jax.ShapeDtypeStruct(features.shape, BF16),
            jax.ShapeDtypeStruct(conv6_weight.shape, F32),
            jax.ShapeDtypeStruct(conv7_weight.shape, F32),
        ),
        in_specs=[hbm] * 6,
        out_specs=(hbm, vmem, vmem),
        scratch_shapes=[
            pltpu.VMEM((FRM, CH), BF16),
            pltpu.VMEM((FRM,), jnp.int32),
            pltpu.SMEM((N_MP,), jnp.int32),
            pltpu.VMEM((N_MP, 4 * UTT, CH), BF16),
            pltpu.VMEM((2, 4, 4, 2, KR, C), BF16),
            pltpu.VMEM((8, FRM), jnp.int32),
            pltpu.VMEM((2, 2 * N_DP, 256), F32),
            pltpu.VMEM((FRM, 4 * CH), BF16),
            pltpu.VMEM((N_DP, BLK, CH), BF16),
            pltpu.VMEM((N_DP, BLK, CH), BF16),
            pltpu.VMEM((2, UTT, 2 * CH), F32),
            pltpu.VMEM((N_MP, UTT, CH), BF16),
            pltpu.VMEM((N_MP, UTT, CH), BF16),
            pltpu.VMEM((N_MP, RC, CH), F32),
            pltpu.VMEM((NCH, 2 * FC, 2 * C), BF16),
            pltpu.VMEM((NCH, FC, 2 * C), BF16),
            pltpu.VMEM((NCH, 2 * FC, C), F32),
            pltpu.VMEM((NCH, FC, C), F32),
            pltpu.VMEM((NCH, FC, C), BF16),
            pltpu.VMEM((NCH, 2 * FC, C), BF16),
            pltpu.VMEM((N_MP, 4 * UTT, CH), BF16),
            pltpu.VMEM((2, 4, 4, 2, KR, C), F32),
            pltpu.VMEM((2, 4, 4, KR, C), BF16),
            pltpu.VMEM((2, 4, 4, KR, C), BF16),
            pltpu.VMEM((2, 4, 4, KR, C), BF16),
            pltpu.VMEM((2, 4, 4, KR, C), BF16),
            pltpu.VMEM((2, 4, KR, C), F32),
            pltpu.VMEM((2, 4, KR, C), BF16),
            pltpu.VMEM((2, 4, KR, C), BF16),
            pltpu.VMEM((2, KR, C), F32),
            pltpu.VMEM((N_MP, 2, KR, CH), F32),
            pltpu.VMEM((N_MP, 2, KR, CH), F32),
            dma((4,)), dma((4,)), dma((4,)), dma((4,)), dma((4,)), dma((4,)), dma((4,)), dma((4,)),
            dma((2, 4)), dma((2, 4)), dma((2, 4)), dma((2, 4)), dma((2,)), dma((2,)),
            dma((6,)), dma((NCH, N_MP)), dma((NCH, N_MP)), dma((N_DP,)), dma((N_DP,)), dma((N_MP,)), dma((N_MP,)),
            dma((NCH, N_MP)), dma((NCH, N_MP)), dma((2,)), dma((2,)), dma((2, 4)), dma((2, 4)), dma((2, 4)), dma((2, 4)),
            dma((N_MP,)), dma((N_MP,)),
        ],
        compiler_params=pltpu.CompilerParams(
            collective_id=0, has_side_effects=True, vmem_limit_bytes=56 * 2**20,
            fuse_transposed_lhs_in_matmul=True,
        ),
        name="encoder_backward",
    )(features, conv6_weight, conv7_weight, frame_grads, frame_dest, lengths)
    return pl.pallas_call(
        hand_over,
        out_shape=tuple(jax.ShapeDtypeStruct(r.shape, r.dtype) for r in results),
        in_specs=[hbm] * 3,
        out_specs=(hbm,) * 3,
        scratch_shapes=[
            pltpu.VMEM((16 * UTT, CH), BF16), pltpu.VMEM((KR, CH), F32), pltpu.VMEM((KR, CH), F32),
            dma((PARTS + 2,)), dma((PARTS + 2,)),
        ],
        name="hand_over",
    )(*results)


def solution(mesh):
    placed = (P("dp", "mp"), P("dp", "mp"), P("dp", "mp"), P("dp", "mp"), P(), P("dp"))
    return jax.shard_map(
        body,
        mesh=mesh,
        in_specs=placed,
        out_specs=(P("dp", "mp"), P("dp", "mp"), P("dp", "mp")),
        check_vma=False,
    )
```
